32 devices in a mesh: ctx: 8 (over y, x, core), tp: 4 (over z).
Axes of the slice: x: 2, y: 2, z: 4, core: 2. Of those that a mesh axis runs over, the one named last changes fastest.
Arguments:
- query: bfloat16 [1024, 4096], P('ctx', 'tp'), may hold values from -6 to 6
- keys: bfloat16 [1024, 4096], P('ctx', 'tp'), may hold values from -6 to 6
- values: bfloat16 [1024, 4096], P('ctx', 'tp'), may hold values from -6 to 6
- residues: float32 [4096, 16], P('tp'), may hold values from -0.078125 to 0.078125
- rates: float32 [4096, 16], P('tp'), may hold values from 0.00029296876 to 0.05
- skip_gain: float32 [4096], P('tp'), may hold values from -4 to 4
- w_out: bfloat16 [4096, 4096], P('tp', 'ctx'), may hold values from -0.125 to 0.125
Outputs:
- mixed: bfloat16 [1024, 4096], P('ctx', 'tp')
The draws below stay inside these ranges and needn't reach their ends.
All inputs are finite; a program needn't handle non-finite values.
Results may differ from the reference program's by a relative error of at most 0.019.
Values may be sent and summed in bfloat16 or wider, within the bound.
A program may use at most 64 MiB of HBM per device.

```python
import math
import jax
import jax.numpy as jnp
from jax import lax

D = 4096
ORDER = 16
TOK_DEV = 128
LENGTH = 1024
N_CTX = 8


def strengthened(values, key, source, target, parts, factor):
    owner, partner = [(jnp.arange(values.shape[dim]) // (values.shape[dim] // parts)).reshape([-1 if axis == dim else 1 for axis in range(values.ndim)]) for dim in (source, target)]
    chosen = jax.random.permutation(key, parts)[partner]
    strong = (owner == chosen) | (owner == (partner + parts // 2) % parts)
    return jnp.where(strong, factor * values, values)


def levels(stream_key, shape, pieces, least, top_value):
    def one(dim, shards_of):
        steps = jax.random.uniform(jax.random.fold_in(jax.random.fold_in(stream_key, 6), dim), (shards_of,), jnp.float32, least / len(pieces), top_value / len(pieces))
        return jnp.repeat(jnp.exp(steps), shape[dim] // shards_of).reshape((-1,) + (1,) * (len(shape) - dim - 1))

    level = one(*pieces[0])
    for cut in pieces[1:]:
        level = level * one(*cut)
    return level


def gaussian(rng, dims, scale, limit, shards=(), kind=jnp.bfloat16):
    factor_of = levels(rng, dims, shards, -0.22, 0.18) if shards else 1.0
    values = jax.random.normal(rng, dims, jnp.float32) * scale * factor_of
    return jnp.minimum(jnp.maximum(values, -limit), limit).astype(kind)


def heavy_noise(stream_key, dims, spread, limit, split, heavy, kind=jnp.bfloat16):
    drawn = spread * jax.random.normal(stream_key, dims, jnp.float32)
    if split:
        drawn = drawn * levels(stream_key, dims, split, -0.22, 0.18)
    return jnp.clip(strengthened(drawn, jax.random.fold_in(stream_key, 3), *heavy), -limit, limit).astype(kind)


def setup_inputs(seed: int = 0) -> dict:
    streams_of = jax.random.split(jax.random.key(seed), 8)
    query = gaussian(streams_of[0], (LENGTH, D), 1.0, 6.0, ((0, 8), (1, 4)))
    keys = gaussian(streams_of[1], (LENGTH, D), 1.0, 6.0, ((0, 8), (1, 4)))
    values = gaussian(streams_of[2], (LENGTH, D), 1.0, 6.0, ((0, 8), (1, 4)))
    residues = gaussian(streams_of[3], (D, ORDER), (2 / (ORDER * TOK_DEV * N_CTX) ** 0.5), 0.078125, ((0, 4),), jnp.float32)
    rates = jnp.clip(jnp.exp(math.log(0.05) - 5.1397123 * jax.random.uniform(streams_of[4], (D, ORDER), jnp.float32) ** levels(streams_of[4], (D, ORDER), ((0, 4),), -0.2, 0.2)), 0.00029296876, 0.05)
    skip_gain = gaussian(streams_of[5], (D,), 1.0, 4.0, ((0, 4),), jnp.float32)
    w_out = heavy_noise(streams_of[6], (D, D), D ** -0.5, 0.125, ((0, 4), (1, 8)), (0, 1, 8, 2.0))
    return {"query": query, "keys": keys, "values": values, "residues": residues, "rates": rates, "skip_gain": skip_gain, "w_out": w_out}


def conv_block(args):
    signal, res, rate = args
    length = signal.shape[0]
    times = jnp.arange(length, dtype=jnp.float32)
    filt = jnp.zeros(signal.shape, jnp.float32)
    for pole in range(res.shape[1]):
        filt = filt + res[None, :, pole] * jnp.exp(-times[:, None] * rate[None, :, pole])
    spec = jnp.fft.rfft(signal, 2 * length, axis=0) * jnp.fft.rfft(filt, 2 * length, axis=0)
    return jnp.fft.irfft(spec, 2 * length, axis=0)[:length].astype(jnp.float32)


def reference(query, keys, values, residues, rates, skip_gain, w_out):
    gated_in = (keys.astype(jnp.float32) * values.astype(jnp.float32)).astype(jnp.bfloat16)
    length = query.shape[0]
    width = query.shape[1]
    block = 64
    blocks = width // block
    signal = gated_in.astype(jnp.float32).reshape(length, blocks, block).transpose(1, 0, 2)
    res = residues.reshape(blocks, block, ORDER)
    rate = rates.reshape(blocks, block, ORDER)
    conv = lax.map(conv_block, (signal, res, rate))
    conv = conv.transpose(1, 0, 2).reshape(length, width).astype(jnp.bfloat16)
    gated = (query.astype(jnp.float32) * (conv.astype(jnp.float32) + skip_gain[None, :] * gated_in.astype(jnp.float32))).astype(jnp.bfloat16)
    return jnp.dot(gated, w_out, preferred_element_type=jnp.float32).astype(jnp.bfloat16)
```

```python
import functools

import jax
import jax.numpy as jnp
from jax import lax
from jax.experimental import pallas as pl
from jax.experimental.pallas import tpu as pltpu
from jax.sharding import PartitionSpec as P

MESH = pl.DeviceIdType.MESH
LANES = 128
F32 = jnp.float32
BF16 = jnp.bfloat16


def spread_channels(dst, value):
    for j in range(value.shape[1] // LANES):
        dst[:, j, :] = value[:, j * LANES : (j + 1) * LANES]


def gate_in(keys, values):
    return (keys[...].astype(F32) * values[...].astype(F32)).astype(BF16)


def run_states(x_ref, lam, start, unroll=8):
    order = lam.shape[0]
    decay = [jnp.exp(-lam[m]) for m in range(order)]

    def body(t, state):
        for u in range(unroll):
            token = x_ref[t * unroll + u]
            state = tuple(decay[m] * state[m] + token for m in range(order))
        return state

    return lax.fori_loop(0, x_ref.shape[0] // unroll, body, start)


def run_conv(x_ref, lam, res, start, unroll=4):
    order = lam.shape[0]
    decay = [jnp.exp(-lam[m]) for m in range(order)]

    def body(t, state):
        for u in range(unroll):
            token = x_ref[t * unroll + u]
            state = tuple(decay[m] * state[m] + token for m in range(order))
            sums = [res[m] * state[m] for m in range(order)]
            while len(sums) > 1:
                sums = [sums[i] + sums[i + 1] for i in range(0, len(sums) - 1, 2)] + (
                    [sums[-1]] if len(sums) % 2 else []
                )
            x_ref[t * unroll + u] = sums[0]
        return state

    lax.fori_loop(0, x_ref.shape[0] // unroll, body, start)


def gate_out(dst, q_ref, k_ref, v_ref, skip_ref, y_ref):
    for j in range(q_ref.shape[1] // LANES):
        cols = pl.ds(j * LANES, LANES)
        gated_in = (k_ref[:, cols].astype(F32) * v_ref[:, cols].astype(F32)).astype(BF16)
        conv = y_ref[:, j, :].astype(BF16).astype(F32)
        total = conv + skip_ref[:, cols] * gated_in.astype(F32)
        dst[:, cols] = (q_ref[:, cols].astype(F32) * total).astype(BF16)


def flip(number, bits):
    for b in range(bits.bit_length()):
        if bits >> b & 1:
            number = number + (1 << b) - 2 * (1 << b) * (number // (1 << b) % 2)
    return number


def fused_kernel(
    n, tp, q_ref, k_ref, v_ref, res_ref, rate_ref, skip_ref, w_ref, out_ref,
    x_ref, lam, res, s_own, s_in, s_give, s_got, gated, share, cols_in, sums_in,
    s_send, s_recv, c_send, c_recv, g_send, g_recv, f_send, p_send, p_recv, z_send, z_recv,
):
    me = lax.axis_index("ctx")
    row = lax.axis_index("tp")
    core = me % 2
    chip = me // 2
    sib = me + 1 - 2 * core
    chips = n // 2
    per_tp = n // tp
    tok = q_ref.shape[0]
    order = lam.shape[0]
    shape = lam.shape[1:]

    barrier = pltpu.get_barrier_semaphore()
    for d in range(1, n):
        pl.semaphore_signal(barrier, inc=1, device_id={"ctx": (me + d) % n}, device_id_type=MESH)
    for d in range(1, tp):
        pl.semaphore_signal(barrier, inc=1, device_id={"tp": (row + d) % tp}, device_id_type=MESH)

    spread_channels(x_ref, gate_in(k_ref, v_ref).astype(F32))
    spread_channels(lam, rate_ref[...].T)
    spread_channels(res, res_ref[...].T)
    zero = tuple(jnp.zeros(shape, F32) for _ in range(order))
    state = run_states(x_ref, lam, zero)
    for m in range(order):
        s_own[m] = state[m]

    pl.semaphore_wait(barrier, n - 1 + tp - 1)

    def over(axis, index, src, dst, send, recv):
        return pltpu.make_async_remote_copy(
            src_ref=src, dst_ref=dst, send_sem=send, recv_sem=recv,
            device_id={axis: index}, device_id_type=MESH,
        )

    def state_copy(d, slot):
        return over("ctx", flip(chip, d) * 2 + core, s_own, s_in.at[slot], s_send.at[d], s_recv.at[slot])

    for d in range(1, chips):
        state_copy(d, chip).start()
    for d in range(1, chips):
        state_copy(d, flip(chip, d)).wait_recv()

    def carry_for(target, dst):
        def weight(source):
            steps = (jnp.maximum(target - 1 - source, 0) * tok).astype(F32)
            live = jnp.where(source < target, 1.0, 0.0).astype(F32)
            return steps, live

        weights = [weight(me)] + [weight(flip(chip, d) * 2 + core) for d in range(1, chips)]
        for m in range(order):
            total = jnp.zeros(shape, F32)
            for d in range(chips):
                part = s_own[m] if d == 0 else s_in[flip(chip, d), m]
                total = total + jnp.exp(-lam[m] * weights[d][0]) * weights[d][1] * part
            dst[m] = total

    carry_for(sib, s_give)
    carry_copy = over("ctx", sib, s_give, s_got, c_send, c_recv)
    carry_copy.start()
    carry_for(me, s_in.at[chip])
    carry_copy.wait_recv()
    run_conv(x_ref, lam, res, tuple(s_in[chip, m] + s_got[m] for m in range(order)))
    gate_out(gated.at[me], q_ref, k_ref, v_ref, skip_ref, x_ref)

    def gated_copy(index, slot, send):
        return over("ctx", index, gated.at[slot], gated.at[slot], send, g_recv.at[slot])

    def product(i):
        return jnp.dot(gated[i], w_ref[...], preferred_element_type=F32).astype(BF16)

    def back_copy(i, slot):
        return over("ctx", i, share.at[i], cols_in.at[slot], p_send.at[i], p_recv.at[slot])

    def sum_copy(k, source):
        return over(
            "tp", k // per_tp, cols_in.at[k], sums_in.at[source, k % per_tp],
            z_send.at[k], z_recv.at[source, k % per_tp],
        )

    def send_back(i):
        share[i] = product(i)
        back_copy(i, me).start()

    def send_on(k):
        @pl.when(k // per_tp != row)
        def _():
            sum_copy(k, row).start()

    def same_core(d):
        return flip(chip, d) * 2 + core

    def other_core(d):
        return flip(chip, d) * 2 + 1 - core

    gated_copy(sib, me, g_send.at[0]).start()
    for d in range(1, chips):
        gated_copy(same_core(d), me, g_send.at[d]).start()
    cols_in[me] = product(me)
    send_on(me)
    gated_copy(sib, sib, g_send.at[0]).wait_recv()
    send_back(sib)
    for d in range(1, chips):
        i = same_core(d)
        gated_copy(i, i, g_send.at[d]).wait_recv()
        gated_copy(sib, i, f_send.at[d]).start()
        send_back(i)
    back_copy(sib, sib).wait_recv()
    send_on(sib)
    for d in range(1, chips):
        i = other_core(d)
        gated_copy(sib, i, f_send.at[d]).wait_recv()
        send_back(i)
        k = same_core(d)
        back_copy(k, k).wait_recv()
        send_on(k)
    for d in range(1, chips):
        k = other_core(d)
        back_copy(k, k).wait_recv()
        send_on(k)

    width = w_ref.shape[1]
    for h in range(per_tp):
        total = cols_in[row * per_tp + h].astype(F32)
        for d in range(1, tp):
            source = (row + d) % tp
            sum_copy(row * per_tp + h, source).wait_recv()
            total = total + sums_in[source, h].astype(F32)
        out_ref[:, pl.ds(h * width, width)] = total.astype(BF16)

    carry_copy.wait_send()
    gated_copy(sib, me, g_send.at[0]).wait_send()
    for d in range(1, chips):
        state_copy(d, chip).wait_send()
        gated_copy(same_core(d), me, g_send.at[d]).wait_send()
        gated_copy(sib, same_core(d), f_send.at[d]).wait_send()
    for d in range(1, n):
        back_copy((me + d) % n, me).wait_send()
    for k in range(n):
        @pl.when(k // per_tp != row)
        def _():
            sum_copy(k, row).wait_send()


def fused(n, tp, query, keys, values, residues, rates, skip_gain, w_out):
    tok, chans = query.shape
    order = residues.shape[1]
    width = w_out.shape[1]
    per_tp = n // tp
    poles = (order, chans // LANES, LANES)
    dma = pltpu.SemaphoreType.DMA
    return pl.pallas_call(
        functools.partial(fused_kernel, n, tp),
        out_shape=jax.ShapeDtypeStruct((tok, per_tp * width), BF16),
        in_specs=[pl.BlockSpec(memory_space=pltpu.VMEM)] * 7,
        out_specs=pl.BlockSpec(memory_space=pltpu.VMEM),
        scratch_shapes=[
            pltpu.VMEM((tok,) + poles[1:], F32),
            pltpu.VMEM(poles, F32),
            pltpu.VMEM(poles, F32),
            pltpu.VMEM(poles, F32),
            pltpu.VMEM((n // 2,) + poles, F32),
            pltpu.VMEM(poles, F32),
            pltpu.VMEM(poles, F32),
            pltpu.VMEM((n, tok, chans), BF16),
            pltpu.VMEM((n, tok, width), BF16),
            pltpu.VMEM((n, tok, width), BF16),
            pltpu.VMEM((tp, per_tp, tok, width), BF16),
            dma((n // 2,)), dma((n // 2,)), dma, dma, dma((n // 2,)), dma((n,)), dma((n // 2,)),
            dma((n,)), dma((n,)), dma((n,)), dma((tp, per_tp)),
        ],
        compiler_params=pltpu.CompilerParams(
            collective_id=0, has_side_effects=True, vmem_limit_bytes=40 * 2**20
        ),
    )(query, keys, values, residues, rates, skip_gain[None, :], w_out)


def states_kernel(k_ref, v_ref, rate_ref, s_ref, x_ref, lam):
    spread_channels(x_ref, gate_in(k_ref, v_ref).astype(F32))
    spread_channels(lam, rate_ref[...].T)
    zero = tuple(jnp.zeros(lam.shape[1:], F32) for _ in range(lam.shape[0]))
    state = run_states(x_ref, lam, zero)
    for m in range(lam.shape[0]):
        s_ref[m] = state[m]


def conv_kernel(q_ref, k_ref, v_ref, res_ref, rate_ref, skip_ref, s_ref, out_ref, x_ref, lam, res):
    spread_channels(x_ref, gate_in(k_ref, v_ref).astype(F32))
    spread_channels(lam, rate_ref[...].T)
    spread_channels(res, res_ref[...].T)
    run_conv(x_ref, lam, res, tuple(s_ref[m] for m in range(lam.shape[0])))
    gate_out(out_ref, q_ref, k_ref, v_ref, skip_ref, x_ref)


def gathered(n, query, keys, values, residues, rates, skip_gain, w_out):
    tok, chans = query.shape
    order = residues.shape[1]
    poles = (order, chans // LANES, LANES)
    block = (tok,) + poles[1:]
    vmem = pl.BlockSpec(memory_space=pltpu.VMEM)
    state = pl.pallas_call(
        states_kernel,
        out_shape=jax.ShapeDtypeStruct(poles, F32),
        in_specs=[vmem] * 3,
        out_specs=vmem,
        scratch_shapes=[pltpu.VMEM(block, F32), pltpu.VMEM(poles, F32)],
        compiler_params=pltpu.CompilerParams(vmem_limit_bytes=24 * 2**20),
    )(keys, values, rates)
    me = lax.axis_index("ctx")
    lam = rates.T.reshape(poles)
    blocks = lax.all_gather(state, "ctx")
    away = me - 1 - jnp.arange(n, dtype=jnp.int32)
    steps = (jnp.maximum(away, 0) * tok).astype(F32)[:, None, None, None]
    live = (away >= 0)[:, None, None, None]
    carry = jnp.sum(jnp.where(live, jnp.exp(-lam[None] * steps) * blocks, 0.0), axis=0)
    gated = pl.pallas_call(
        conv_kernel,
        out_shape=jax.ShapeDtypeStruct((tok, chans), BF16),
        in_specs=[vmem] * 7,
        out_specs=vmem,
        scratch_shapes=[pltpu.VMEM(block, F32), pltpu.VMEM(poles, F32), pltpu.VMEM(poles, F32)],
        compiler_params=pltpu.CompilerParams(vmem_limit_bytes=24 * 2**20),
    )(query, keys, values, residues, rates, skip_gain[None, :], carry)
    weights = lax.all_gather(w_out, "ctx", axis=1, tiled=True)
    part = jnp.dot(gated, weights, preferred_element_type=F32).astype(BF16)
    return lax.psum_scatter(part, "tp", scatter_dimension=1, tiled=True)


def solution(mesh):
    n, tp = mesh.shape["ctx"], mesh.shape["tp"]

    def per_device(query, keys, values, residues, rates, skip_gain, w_out):
        args = (query, keys, values, residues, rates, skip_gain, w_out)
        few_tokens = n * query.shape[0] <= tp * query.shape[1]
        even = n & (n - 1) == 0 and n > 1 and n % tp == 0 and w_out.shape[1] % LANES == 0
        if few_tokens and even:
            return fused(n, tp, *args)
        return gathered(n, *args)

    placed = (
        P("ctx", "tp"),
        P("ctx", "tp"),
        P("ctx", "tp"),
        P("tp", None),
        P("tp", None),
        P("tp"),
        P("tp", "ctx"),
    )
    return jax.shard_map(
        per_device, mesh=mesh, in_specs=placed, out_specs=P("ctx", "tp"), check_vma=False
    )
```

```python
import functools

import jax
import jax.numpy as jnp
from jax import lax
from jax.experimental import pallas as pl
from jax.experimental.pallas import tpu as pltpu
from jax.sharding import PartitionSpec as P

MESH = pl.DeviceIdType.MESH
LANES = 128
F32 = jnp.float32
BF16 = jnp.bfloat16


def spread_channels(dst, value):
    for j in range(value.shape[1] // LANES):
        dst[:, j, :] = value[:, j * LANES : (j + 1) * LANES]


def gate_in(keys, values):
    return (keys[...].astype(F32) * values[...].astype(F32)).astype(BF16)


def tree_sum(terms):
    terms = list(terms)
    while len(terms) > 1:
        odd = [terms[-1]] if len(terms) % 2 else []
        terms = [terms[i] + terms[i + 1] for i in range(0, len(terms) - 1, 2)] + odd
    return terms[0]


def run_states(x_ref, lam, start, unroll=8):
    order = lam.shape[0]
    decay = [jnp.exp(-lam[m]) for m in range(order)]

    def body(t, state):
        for u in range(unroll):
            token = x_ref[t * unroll + u]
            state = tuple(decay[m] * state[m] + token for m in range(order))
        return state

    return lax.fori_loop(0, x_ref.shape[0] // unroll, body, start)


def run_conv(x_ref, lam, res, start, unroll=4):
    order = lam.shape[0]
    decay = [jnp.exp(-lam[m]) for m in range(order)]

    def body(t, state):
        for u in range(unroll):
            token = x_ref[t * unroll + u]
            state = tuple(decay[m] * state[m] + token for m in range(order))
            x_ref[t * unroll + u] = tree_sum([res[m] * state[m] for m in range(order)])
        return state

    lax.fori_loop(0, x_ref.shape[0] // unroll, body, start)


def add_carry(y_ref, lam, start, unroll=8):
    order = lam.shape[0]
    decay = [jnp.exp(-lam[m]) for m in range(order)]

    def body(t, state):
        for u in range(unroll):
            state = tuple(decay[m] * state[m] for m in range(order))
            y_ref[t * unroll + u] = y_ref[t * unroll + u] + tree_sum(state)
        return state

    lax.fori_loop(0, y_ref.shape[0] // unroll, body, start)


def gate_out(dst, q_ref, k_ref, v_ref, skip_ref, y_ref):
    for j in range(q_ref.shape[1] // LANES):
        cols = pl.ds(j * LANES, LANES)
        gated_in = (k_ref[:, cols].astype(F32) * v_ref[:, cols].astype(F32)).astype(BF16)
        conv = y_ref[:, j, :].astype(BF16).astype(F32)
        total = conv + skip_ref[:, cols] * gated_in.astype(F32)
        dst[:, cols] = (q_ref[:, cols].astype(F32) * total).astype(BF16)


def flip(number, bits):
    for b in range(bits.bit_length()):
        if bits >> b & 1:
            number = number + (1 << b) - 2 * (1 << b) * (number // (1 << b) % 2)
    return number


def fused_kernel(
    n, tp, q_hbm, k_hbm, v_hbm, res_hbm, rate_hbm, skip_hbm, w_hbm, out_ref,
    q_ref, k_ref, v_ref, res_ref, rate_ref, skip_ref, w_ref,
    x_ref, lam, res, s_own, s_in, s_give, s_got, gated, share, cols_in, from_low, from_high,
    load, s_send, s_recv, c_send, c_recv, g_send, g_recv, f_send, h_send, h_recv,
    p_send, p_recv, z_send, low_recv, high_recv,
):
    me = lax.axis_index("ctx")
    row = lax.axis_index("tp")
    core = me % 2
    chip = me // 2
    sib = me + 1 - 2 * core
    chips = n // 2
    per_tp = n // tp
    tok = q_ref.shape[0]
    half = tok // 2
    order = lam.shape[0]
    shape = lam.shape[1:]

    pairs = (
        (k_hbm, k_ref), (v_hbm, v_ref), (rate_hbm, rate_ref), (res_hbm, res_ref),
        (q_hbm, q_ref), (skip_hbm, skip_ref), (w_hbm, w_ref),
    )
    loads = [pltpu.make_async_copy(src, dst, load.at[i]) for i, (src, dst) in enumerate(pairs)]
    for copy in loads:
        copy.start()

    barrier = pltpu.get_barrier_semaphore()
    for d in range(1, n):
        pl.semaphore_signal(barrier, inc=1, device_id={"ctx": (me + d) % n}, device_id_type=MESH)

    @pl.when(row > 0)
    def _():
        pl.semaphore_signal(barrier, inc=1, device_id={"tp": row - 1}, device_id_type=MESH)

    @pl.when(row < tp - 1)
    def _():
        pl.semaphore_signal(barrier, inc=1, device_id={"tp": row + 1}, device_id_type=MESH)

    for copy in loads[:3]:
        copy.wait()
    spread_channels(x_ref, gate_in(k_ref, v_ref).astype(F32))
    spread_channels(lam, rate_ref[...])
    zero = tuple(jnp.zeros(shape, F32) for _ in range(order))
    state = run_states(x_ref, lam, zero)
    for m in range(order):
        s_own[m] = state[m]

    neighbours = jnp.where(row > 0, 1, 0) + jnp.where(row < tp - 1, 1, 0)
    pl.semaphore_wait(barrier, n - 1 + neighbours)

    def over(axis, index, src, dst, send, recv):
        return pltpu.make_async_remote_copy(
            src_ref=src, dst_ref=dst, send_sem=send, recv_sem=recv,
            device_id={axis: index}, device_id_type=MESH,
        )

    def state_copy(d, slot):
        return over("ctx", flip(chip, d) * 2 + core, s_own, s_in.at[slot], s_send.at[d], s_recv.at[slot])

    for d in range(1, chips):
        state_copy(d, chip).start()
    loads[3].wait()
    spread_channels(res, res_ref[...])
    run_conv(x_ref, lam, res, zero)
    for copy in loads[4:]:
        copy.wait()
    for d in range(1, chips):
        state_copy(d, flip(chip, d)).wait_recv()

    def carry_for(target, dst):
        def weight(source):
            steps = (jnp.maximum(target - 1 - source, 0) * tok).astype(F32)
            live = jnp.where(source < target, 1.0, 0.0).astype(F32)
            return steps, live

        weights = [weight(me)] + [weight(flip(chip, d) * 2 + core) for d in range(1, chips)]
        for m in range(order):
            total = jnp.zeros(shape, F32)
            for d in range(chips):
                part = s_own[m] if d == 0 else s_in[flip(chip, d), m]
                total = total + jnp.exp(-lam[m] * weights[d][0]) * weights[d][1] * part
            dst[m] = total

    carry_for(sib, s_give)
    carry_copy = over("ctx", sib, s_give, s_got, c_send, c_recv)
    carry_copy.start()
    carry_for(me, s_in.at[chip])
    carry_copy.wait_recv()
    add_carry(x_ref, lam, tuple(res[m] * (s_in[chip, m] + s_got[m]) for m in range(order)))
    gate_out(gated.at[me], q_ref, k_ref, v_ref, skip_ref, x_ref)

    def same_core(d):
        return flip(chip, d) * 2 + core

    def other_core(d):
        return flip(chip, d) * 2 + 1 - core

    def gated_copy(index, slot, send):
        return over("ctx", index, gated.at[slot], gated.at[slot], send, g_recv.at[slot])

    def half_copy(index, slot, part):
        rows = pl.ds(part * half, half)
        return over(
            "ctx", index, gated.at[slot, rows], gated.at[slot, rows], h_send.at[part], h_recv.at[part]
        )

    def product(i):
        return jnp.dot(gated[i], w_ref[...], preferred_element_type=F32).astype(BF16)

    def back_copy(i, slot):
        return over("ctx", i, share.at[i], cols_in.at[slot], p_send.at[i], p_recv.at[slot])

    def down_copy(k):
        return over("tp", (row + tp - 1) % tp, cols_in.at[k], from_high.at[k], z_send.at[k], high_recv.at[k])

    def up_copy(k):
        return over("tp", (row + 1) % tp, cols_in.at[k], from_low.at[k], z_send.at[k], low_recv.at[k])

    def send_back(i):
        share[i] = product(i)
        back_copy(i, me).start()

    def send_on(k):
        target = k // per_tp

        @pl.when(row > target)
        def _():
            @pl.when(row < tp - 1)
            def _():
                down_copy(k).wait_recv()
                cols_in[k] = (cols_in[k].astype(F32) + from_high[k].astype(F32)).astype(BF16)

            down_copy(k).start()

        @pl.when(row < target)
        def _():
            @pl.when(row > 0)
            def _():
                up_copy(k).wait_recv()
                cols_in[k] = (cols_in[k].astype(F32) + from_low[k].astype(F32)).astype(BF16)

            up_copy(k).start()

    def arrived(k):
        back_copy(k, k).wait_recv()
        send_on(k)

    def take_other(d):
        i = other_core(d)
        gated_copy(sib, i, f_send.at[d]).wait_recv()
        send_back(i)

    gated_copy(same_core(1), me, g_send.at[1]).start()
    gated_copy(same_core(2), me, g_send.at[2]).start()
    gated_copy(sib, me, g_send.at[0]).start()
    cols_in[me] = product(me)
    gated_copy(sib, sib, g_send.at[0]).wait_recv()
    send_back(sib)
    send_on(me)
    for d in (1, 2):
        i = same_core(d)
        gated_copy(i, i, g_send.at[d]).wait_recv()
        half_copy(same_core(3 - d), i, 2 - d).start()
        gated_copy(sib, i, f_send.at[d]).start()
        send_back(i)
    arrived(sib)
    take_other(1)
    take_other(2)
    arrived(same_core(1))
    arrived(same_core(2))
    far = same_core(3)
    half_copy(me, far, 0).wait_recv()
    half_copy(me, far, 1).wait_recv()
    gated_copy(sib, far, f_send.at[3]).start()
    send_back(far)
    arrived(other_core(1))
    take_other(3)
    arrived(other_core(2))
    arrived(far)
    arrived(other_core(3))

    width = w_ref.shape[1]
    for h in range(per_tp):
        k = row * per_tp + h
        cols = pl.ds(h * width, width)

        @pl.when(row == 0)
        def _():
            down_copy(k).wait_recv()
            out_ref[:, cols] = (cols_in[k].astype(F32) + from_high[k].astype(F32)).astype(BF16)

        @pl.when(row == tp - 1)
        def _():
            up_copy(k).wait_recv()
            out_ref[:, cols] = (cols_in[k].astype(F32) + from_low[k].astype(F32)).astype(BF16)

        @pl.when((row > 0) & (row < tp - 1))
        def _():
            down_copy(k).wait_recv()
            up_copy(k).wait_recv()
            both = from_low[k].astype(F32) + from_high[k].astype(F32)
            out_ref[:, cols] = (cols_in[k].astype(F32) + both).astype(BF16)

    carry_copy.wait_send()
    gated_copy(sib, me, g_send.at[0]).wait_send()
    for d in range(1, chips):
        state_copy(d, chip).wait_send()
        gated_copy(sib, same_core(d), f_send.at[d]).wait_send()
    for d in (1, 2):
        gated_copy(same_core(d), me, g_send.at[d]).wait_send()
        half_copy(same_core(3 - d), same_core(d), 2 - d).wait_send()
    for d in range(1, n):
        back_copy((me + d) % n, me).wait_send()
    for k in range(n):
        @pl.when(k // per_tp != row)
        def _():
            down_copy(k).wait_send()


def fused(n, tp, query, keys, values, residues, rates, skip_gain, w_out):
    tok, chans = query.shape
    order = residues.shape[1]
    width = w_out.shape[1]
    per_tp = n // tp
    poles = (order, chans // LANES, LANES)
    dma = pltpu.SemaphoreType.DMA
    vmem = pltpu.VMEM
    blocks = vmem((n, tok, width), BF16)
    return pl.pallas_call(
        functools.partial(fused_kernel, n, tp),
        out_shape=jax.ShapeDtypeStruct((tok, per_tp * width), BF16),
        in_specs=[pl.BlockSpec(memory_space=pltpu.HBM)] * 7,
        out_specs=pl.BlockSpec(memory_space=pltpu.VMEM),
        scratch_shapes=[
            vmem((tok, chans), BF16), vmem((tok, chans), BF16), vmem((tok, chans), BF16),
            vmem((order, chans), F32), vmem((order, chans), F32), vmem((1, chans), F32),
            vmem((chans, width), BF16),
            vmem((tok,) + poles[1:], F32),
            vmem(poles, F32), vmem(poles, F32), vmem(poles, F32),
            vmem((n // 2,) + poles, F32), vmem(poles, F32), vmem(poles, F32),
            vmem((n, tok, chans), BF16),
            blocks, blocks, blocks, blocks,
            dma((7,)), dma((n // 2,)), dma((n // 2,)), dma, dma, dma((3,)), dma((n,)), dma((n // 2,)),
            dma((2,)), dma((2,)), dma((n,)), dma((n,)), dma((n,)), dma((n,)), dma((n,)),
        ],
        compiler_params=pltpu.CompilerParams(
            collective_id=0, has_side_effects=True, vmem_limit_bytes=60 * 2**20
        ),
    )(query, keys, values, residues.T, rates.T, skip_gain[None, :], w_out)


def states_kernel(k_ref, v_ref, rate_ref, s_ref, x_ref, lam):
    spread_channels(x_ref, gate_in(k_ref, v_ref).astype(F32))
    spread_channels(lam, rate_ref[...])
    zero = tuple(jnp.zeros(lam.shape[1:], F32) for _ in range(lam.shape[0]))
    state = run_states(x_ref, lam, zero)
    for m in range(lam.shape[0]):
        s_ref[m] = state[m]


def conv_kernel(q_ref, k_ref, v_ref, res_ref, rate_ref, skip_ref, s_ref, out_ref, x_ref, lam, res):
    spread_channels(x_ref, gate_in(k_ref, v_ref).astype(F32))
    spread_channels(lam, rate_ref[...])
    spread_channels(res, res_ref[...])
    run_conv(x_ref, lam, res, tuple(s_ref[m] for m in range(lam.shape[0])))
    gate_out(out_ref, q_ref, k_ref, v_ref, skip_ref, x_ref)


def gathered(n, query, keys, values, residues, rates, skip_gain, w_out):
    tok, chans = query.shape
    order = residues.shape[1]
    poles = (order, chans // LANES, LANES)
    block = (tok,) + poles[1:]
    vmem = pl.BlockSpec(memory_space=pltpu.VMEM)
    state = pl.pallas_call(
        states_kernel,
        out_shape=jax.ShapeDtypeStruct(poles, F32),
        in_specs=[vmem] * 3,
        out_specs=vmem,
        scratch_shapes=[pltpu.VMEM(block, F32), pltpu.VMEM(poles, F32)],
        compiler_params=pltpu.CompilerParams(vmem_limit_bytes=24 * 2**20),
    )(keys, values, rates.T)
    me = lax.axis_index("ctx")
    lam = rates.T.reshape(poles)
    blocks = lax.all_gather(state, "ctx")
    away = me - 1 - jnp.arange(n, dtype=jnp.int32)
    steps = (jnp.maximum(away, 0) * tok).astype(F32)[:, None, None, None]
    live = (away >= 0)[:, None, None, None]
    carry = jnp.sum(jnp.where(live, jnp.exp(-lam[None] * steps) * blocks, 0.0), axis=0)
    gated = pl.pallas_call(
        conv_kernel,
        out_shape=jax.ShapeDtypeStruct((tok, chans), BF16),
        in_specs=[vmem] * 7,
        out_specs=vmem,
        scratch_shapes=[pltpu.VMEM(block, F32), pltpu.VMEM(poles, F32), pltpu.VMEM(poles, F32)],
        compiler_params=pltpu.CompilerParams(vmem_limit_bytes=24 * 2**20),
    )(query, keys, values, residues.T, rates.T, skip_gain[None, :], carry)
    weights = lax.all_gather(w_out, "ctx", axis=1, tiled=True)
    part = jnp.dot(gated, weights, preferred_element_type=F32).astype(BF16)
    return lax.psum_scatter(part, "tp", scatter_dimension=1, tiled=True)


def solution(mesh):
    n, tp = mesh.shape["ctx"], mesh.shape["tp"]

    def per_device(query, keys, values, residues, rates, skip_gain, w_out):
        args = (query, keys, values, residues, rates, skip_gain, w_out)
        few_tokens = n * query.shape[0] <= tp * query.shape[1]
        even = n == 8 and n % tp == 0 and w_out.shape[1] % LANES == 0
        if few_tokens and even:
            return fused(n, tp, *args)
        return gathered(n, *args)

    placed = (
        P("ctx", "tp"),
        P("ctx", "tp"),
        P("ctx", "tp"),
        P("tp", None),
        P("tp", None),
        P("tp"),
        P("tp", "ctx"),
    )
    return jax.shard_map(
        per_device, mesh=mesh, in_specs=placed, out_specs=P("ctx", "tp"), check_vma=False
    )
```

```python
import functools

import jax
import jax.numpy as jnp
from jax import lax
from jax.experimental import pallas as pl
from jax.experimental.pallas import tpu as pltpu
from jax.sharding import PartitionSpec as P

MESH = pl.DeviceIdType.MESH
LANES = 128
F32 = jnp.float32
BF16 = jnp.bfloat16


def spread_channels(dst, value):
    for j in range(value.shape[1] // LANES):
        dst[:, j, :] = value[:, j * LANES : (j + 1) * LANES]


def gate_in(keys, values):
    return (keys[...].astype(F32) * values[...].astype(F32)).astype(BF16)


def tree_sum(terms):
    terms = list(terms)
    while len(terms) > 1:
        odd = [terms[-1]] if len(terms) % 2 else []
        terms = [terms[i] + terms[i + 1] for i in range(0, len(terms) - 1, 2)] + odd
    return terms[0]


def run_states(x_ref, lam, start, unroll=8):
    order = lam.shape[0]
    decay = [jnp.exp(-lam[m]) for m in range(order)]

    def body(t, state):
        for u in range(unroll):
            token = x_ref[t * unroll + u]
            state = tuple(decay[m] * state[m] + token for m in range(order))
        return state

    return lax.fori_loop(0, x_ref.shape[0] // unroll, body, start)


def run_conv(x_ref, lam, res, start, unroll=4):
    order = lam.shape[0]
    decay = [jnp.exp(-lam[m]) for m in range(order)]

    def body(t, state):
        for u in range(unroll):
            token = x_ref[t * unroll + u]
            state = tuple(decay[m] * state[m] + token for m in range(order))
            x_ref[t * unroll + u] = tree_sum([res[m] * state[m] for m in range(order)])
        return state

    lax.fori_loop(0, x_ref.shape[0] // unroll, body, start)


def add_carry(y_ref, lam, start, unroll=8):
    order = lam.shape[0]
    decay = [jnp.exp(-lam[m]) for m in range(order)]

    def body(t, state):
        for u in range(unroll):
            state = tuple(decay[m] * state[m] for m in range(order))
            y_ref[t * unroll + u] = y_ref[t * unroll + u] + tree_sum(state)
        return state

    lax.fori_loop(0, y_ref.shape[0] // unroll, body, start)


def gate_out(dst, q_ref, k_ref, v_ref, skip_ref, y_ref):
    for j in range(q_ref.shape[1] // LANES):
        cols = pl.ds(j * LANES, LANES)
        gated_in = (k_ref[:, cols].astype(F32) * v_ref[:, cols].astype(F32)).astype(BF16)
        conv = y_ref[:, j, :].astype(BF16).astype(F32)
        total = conv + skip_ref[:, cols] * gated_in.astype(F32)
        dst[:, cols] = (q_ref[:, cols].astype(F32) * total).astype(BF16)


def flip(number, bits):
    for b in range(bits.bit_length()):
        if bits >> b & 1:
            number = number + (1 << b) - 2 * (1 << b) * (number // (1 << b) % 2)
    return number


def fused_kernel(
    n, tp, q_hbm, k_hbm, v_hbm, res_hbm, rate_hbm, skip_hbm, w_hbm, out_ref,
    q_ref, k_ref, v_ref, res_ref, rate_ref, skip_ref, w_ref,
    x_ref, lam, res, s_own, s_in, s_give, s_got, gated, share, cols_in, sums_in,
    load, s_send, s_recv, c_send, c_recv, g_send, g_recv, f_send, h_send, h_recv,
    p_send, p_recv, z_send, z_recv,
):
    me = lax.axis_index("ctx")
    row = lax.axis_index("tp")
    core = me % 2
    chip = me // 2
    sib = me + 1 - 2 * core
    chips = n // 2
    per_tp = n // tp
    tok = q_ref.shape[0]
    half = tok // 2
    order = lam.shape[0]
    shape = lam.shape[1:]

    pairs = (
        (k_hbm, k_ref), (v_hbm, v_ref), (rate_hbm, rate_ref), (res_hbm, res_ref),
        (q_hbm, q_ref), (skip_hbm, skip_ref), (w_hbm, w_ref),
    )
    loads = [pltpu.make_async_copy(src, dst, load.at[i]) for i, (src, dst) in enumerate(pairs)]
    for copy in loads:
        copy.start()

    barrier = pltpu.get_barrier_semaphore()
    for d in range(1, n):
        pl.semaphore_signal(barrier, inc=1, device_id={"ctx": (me + d) % n}, device_id_type=MESH)

    for d in range(1, tp):
        pl.semaphore_signal(barrier, inc=1, device_id={"tp": (row + d) % tp}, device_id_type=MESH)

    for copy in loads[:3]:
        copy.wait()
    spread_channels(x_ref, gate_in(k_ref, v_ref).astype(F32))
    spread_channels(lam, rate_ref[...])
    zero = tuple(jnp.zeros(shape, F32) for _ in range(order))
    state = run_states(x_ref, lam, zero)
    for m in range(order):
        s_own[m] = state[m]

    pl.semaphore_wait(barrier, n - 1 + tp - 1)

    def over(axis, index, src, dst, send, recv):
        return pltpu.make_async_remote_copy(
            src_ref=src, dst_ref=dst, send_sem=send, recv_sem=recv,
            device_id={axis: index}, device_id_type=MESH,
        )

    def state_copy(d, slot):
        return over("ctx", flip(chip, d) * 2 + core, s_own, s_in.at[slot], s_send.at[d], s_recv.at[slot])

    for d in range(1, chips):
        state_copy(d, chip).start()
    loads[3].wait()
    spread_channels(res, res_ref[...])
    run_conv(x_ref, lam, res, zero)
    for copy in loads[4:]:
        copy.wait()
    for d in range(1, chips):
        state_copy(d, flip(chip, d)).wait_recv()

    def carry_for(target, dst):
        def weight(source):
            steps = (jnp.maximum(target - 1 - source, 0) * tok).astype(F32)
            live = jnp.where(source < target, 1.0, 0.0).astype(F32)
            return steps, live

        weights = [weight(me)] + [weight(flip(chip, d) * 2 + core) for d in range(1, chips)]
        for m in range(order):
            total = jnp.zeros(shape, F32)
            for d in range(chips):
                part = s_own[m] if d == 0 else s_in[flip(chip, d), m]
                total = total + jnp.exp(-lam[m] * weights[d][0]) * weights[d][1] * part
            dst[m] = total

    carry_for(sib, s_give)
    carry_copy = over("ctx", sib, s_give, s_got, c_send, c_recv)
    carry_copy.start()
    carry_for(me, s_in.at[chip])
    carry_copy.wait_recv()
    add_carry(x_ref, lam, tuple(res[m] * (s_in[chip, m] + s_got[m]) for m in range(order)))
    gate_out(gated.at[me], q_ref, k_ref, v_ref, skip_ref, x_ref)

    def same_core(d):
        return flip(chip, d) * 2 + core

    def other_core(d):
        return flip(chip, d) * 2 + 1 - core

    def gated_copy(index, slot, send):
        return over("ctx", index, gated.at[slot], gated.at[slot], send, g_recv.at[slot])

    def half_copy(index, slot, part):
        rows = pl.ds(part * half, half)
        return over(
            "ctx", index, gated.at[slot, rows], gated.at[slot, rows], h_send.at[part], h_recv.at[part]
        )

    def product(i):
        return jnp.dot(gated[i], w_ref[...], preferred_element_type=F32).astype(BF16)

    def back_copy(i, slot):
        return over("ctx", i, share.at[i], cols_in.at[slot], p_send.at[i], p_recv.at[slot])

    def sum_copy(k, source):
        return over(
            "tp", k // per_tp, cols_in.at[k], sums_in.at[source, k % per_tp],
            z_send.at[k], z_recv.at[source, k % per_tp],
        )

    def send_back(i):
        share[i] = product(i)
        back_copy(i, me).start()

    def send_on(k):
        @pl.when(k // per_tp != row)
        def _():
            sum_copy(k, row).start()

    def arrived(k):
        back_copy(k, k).wait_recv()
        send_on(k)

    def take_other(d):
        i = other_core(d)
        gated_copy(sib, i, f_send.at[d]).wait_recv()
        send_back(i)

    gated_copy(same_core(1), me, g_send.at[1]).start()
    gated_copy(same_core(2), me, g_send.at[2]).start()
    gated_copy(sib, me, g_send.at[0]).start()
    cols_in[me] = product(me)
    gated_copy(sib, sib, g_send.at[0]).wait_recv()
    send_back(sib)
    send_on(me)
    for d in (1, 2):
        i = same_core(d)
        gated_copy(i, i, g_send.at[d]).wait_recv()
        half_copy(same_core(3 - d), i, 2 - d).start()
        gated_copy(sib, i, f_send.at[d]).start()
        send_back(i)
    arrived(sib)
    take_other(1)
    take_other(2)
    arrived(same_core(1))
    far = same_core(3)
    half_copy(me, far, 0).wait_recv()
    half_copy(me, far, 1).wait_recv()
    gated_copy(sib, far, f_send.at[3]).start()
    send_back(far)
    arrived(same_core(2))
    take_other(3)
    arrived(other_core(1))
    arrived(other_core(2))
    arrived(far)
    arrived(other_core(3))

    width = w_ref.shape[1]
    for h in range(per_tp):
        total = cols_in[row * per_tp + h].astype(F32)
        for d in range(1, tp):
            source = (row + d) % tp
            sum_copy(row * per_tp + h, source).wait_recv()
            total = total + sums_in[source, h].astype(F32)
        out_ref[:, pl.ds(h * width, width)] = total.astype(BF16)

    carry_copy.wait_send()
    gated_copy(sib, me, g_send.at[0]).wait_send()
    for d in range(1, chips):
        state_copy(d, chip).wait_send()
        gated_copy(sib, same_core(d), f_send.at[d]).wait_send()
    for d in (1, 2):
        gated_copy(same_core(d), me, g_send.at[d]).wait_send()
        half_copy(same_core(3 - d), same_core(d), 2 - d).wait_send()
    for d in range(1, n):
        back_copy((me + d) % n, me).wait_send()
    for k in range(n):
        @pl.when(k // per_tp != row)
        def _():
            sum_copy(k, row).wait_send()


def fused(n, tp, query, keys, values, residues, rates, skip_gain, w_out):
    tok, chans = query.shape
    order = residues.shape[1]
    width = w_out.shape[1]
    per_tp = n // tp
    poles = (order, chans // LANES, LANES)
    dma = pltpu.SemaphoreType.DMA
    vmem = pltpu.VMEM
    blocks = vmem((n, tok, width), BF16)
    return pl.pallas_call(
        functools.partial(fused_kernel, n, tp),
        out_shape=jax.ShapeDtypeStruct((tok, per_tp * width), BF16),
        in_specs=[pl.BlockSpec(memory_space=pltpu.HBM)] * 7,
        out_specs=pl.BlockSpec(memory_space=pltpu.VMEM),
        scratch_shapes=[
            vmem((tok, chans), BF16), vmem((tok, chans), BF16), vmem((tok, chans), BF16),
            vmem((order, chans), F32), vmem((order, chans), F32), vmem((1, chans), F32),
            vmem((chans, width), BF16),
            vmem((tok,) + poles[1:], F32),
            vmem(poles, F32), vmem(poles, F32), vmem(poles, F32),
            vmem((n // 2,) + poles, F32), vmem(poles, F32), vmem(poles, F32),
            vmem((n, tok, chans), BF16),
            blocks, blocks, vmem((tp, per_tp, tok, width), BF16),
            dma((7,)), dma((n // 2,)), dma((n // 2,)), dma, dma, dma((3,)), dma((n,)), dma((n // 2,)),
            dma((2,)), dma((2,)), dma((n,)), dma((n,)), dma((n,)), dma((tp, per_tp)),
        ],
        compiler_params=pltpu.CompilerParams(
            collective_id=0, has_side_effects=True, vmem_limit_bytes=60 * 2**20
        ),
    )(query, keys, values, residues.T, rates.T, skip_gain[None, :], w_out)


def states_kernel(k_ref, v_ref, rate_ref, s_ref, x_ref, lam):
    spread_channels(x_ref, gate_in(k_ref, v_ref).astype(F32))
    spread_channels(lam, rate_ref[...])
    zero = tuple(jnp.zeros(lam.shape[1:], F32) for _ in range(lam.shape[0]))
    state = run_states(x_ref, lam, zero)
    for m in range(lam.shape[0]):
        s_ref[m] = state[m]


def conv_kernel(q_ref, k_ref, v_ref, res_ref, rate_ref, skip_ref, s_ref, out_ref, x_ref, lam, res):
    spread_channels(x_ref, gate_in(k_ref, v_ref).astype(F32))
    spread_channels(lam, rate_ref[...])
    spread_channels(res, res_ref[...])
    run_conv(x_ref, lam, res, tuple(s_ref[m] for m in range(lam.shape[0])))
    gate_out(out_ref, q_ref, k_ref, v_ref, skip_ref, x_ref)


def gathered(n, query, keys, values, residues, rates, skip_gain, w_out):
    tok, chans = query.shape
    order = residues.shape[1]
    poles = (order, chans // LANES, LANES)
    block = (tok,) + poles[1:]
    vmem = pl.BlockSpec(memory_space=pltpu.VMEM)
    state = pl.pallas_call(
        states_kernel,
        out_shape=jax.ShapeDtypeStruct(poles, F32),
        in_specs=[vmem] * 3,
        out_specs=vmem,
        scratch_shapes=[pltpu.VMEM(block, F32), pltpu.VMEM(poles, F32)],
        compiler_params=pltpu.CompilerParams(vmem_limit_bytes=24 * 2**20),
    )(keys, values, rates.T)
    me = lax.axis_index("ctx")
    lam = rates.T.reshape(poles)
    blocks = lax.all_gather(state, "ctx")
    away = me - 1 - jnp.arange(n, dtype=jnp.int32)
    steps = (jnp.maximum(away, 0) * tok).astype(F32)[:, None, None, None]
    live = (away >= 0)[:, None, None, None]
    carry = jnp.sum(jnp.where(live, jnp.exp(-lam[None] * steps) * blocks, 0.0), axis=0)
    gated = pl.pallas_call(
        conv_kernel,
        out_shape=jax.ShapeDtypeStruct((tok, chans), BF16),
        in_specs=[vmem] * 7,
        out_specs=vmem,
        scratch_shapes=[pltpu.VMEM(block, F32), pltpu.VMEM(poles, F32), pltpu.VMEM(poles, F32)],
        compiler_params=pltpu.CompilerParams(vmem_limit_bytes=24 * 2**20),
    )(query, keys, values, residues.T, rates.T, skip_gain[None, :], carry)
    weights = lax.all_gather(w_out, "ctx", axis=1, tiled=True)
    part = jnp.dot(gated, weights, preferred_element_type=F32).astype(BF16)
    return lax.psum_scatter(part, "tp", scatter_dimension=1, tiled=True)


def solution(mesh):
    n, tp = mesh.shape["ctx"], mesh.shape["tp"]

    def per_device(query, keys, values, residues, rates, skip_gain, w_out):
        args = (query, keys, values, residues, rates, skip_gain, w_out)
        few_tokens = n * query.shape[0] <= tp * query.shape[1]
        even = n == 8 and n % tp == 0 and w_out.shape[1] % LANES == 0
        if few_tokens and even:
            return fused(n, tp, *args)
        return gathered(n, *args)

    placed = (
        P("ctx", "tp"),
        P("ctx", "tp"),
        P("ctx", "tp"),
        P("tp", None),
        P("tp", None),
        P("tp"),
        P("tp", "ctx"),
    )
    return jax.shard_map(
        per_device, mesh=mesh, in_specs=placed, out_specs=P("ctx", "tp"), check_vma=False
    )
```

```python
import functools

import jax
import jax.numpy as jnp
from jax import lax
from jax.experimental import pallas as pl
from jax.experimental.pallas import tpu as pltpu
from jax.sharding import PartitionSpec as P

MESH = pl.DeviceIdType.MESH
LANES = 128
F32 = jnp.float32
BF16 = jnp.bfloat16


def spread_channels(dst, value):
    for j in range(value.shape[1] // LANES):
        dst[:, j, :] = value[:, j * LANES : (j + 1) * LANES]


def gate_in(keys, values):
    return (keys[...].astype(F32) * values[...].astype(F32)).astype(BF16)


def tree_sum(terms):
    terms = list(terms)
    while len(terms) > 1:
        odd = [terms[-1]] if len(terms) % 2 else []
        terms = [terms[i] + terms[i + 1] for i in range(0, len(terms) - 1, 2)] + odd
    return terms[0]


def run_states(x_ref, lam, start, unroll=8):
    order = lam.shape[0]
    decay = [jnp.exp(-lam[m]) for m in range(order)]

    def body(t, state):
        for u in range(unroll):
            token = x_ref[t * unroll + u]
            state = tuple(decay[m] * state[m] + token for m in range(order))
        return state

    return lax.fori_loop(0, x_ref.shape[0] // unroll, body, start)


def run_conv(x_ref, lam, res, start, unroll=4):
    order = lam.shape[0]
    decay = [jnp.exp(-lam[m]) for m in range(order)]

    def body(t, state):
        for u in range(unroll):
            token = x_ref[t * unroll + u]
            state = tuple(decay[m] * state[m] + token for m in range(order))
            x_ref[t * unroll + u] = tree_sum([res[m] * state[m] for m in range(order)])
        return state

    lax.fori_loop(0, x_ref.shape[0] // unroll, body, start)


def add_carry(y_ref, lam, start, unroll=8):
    order = lam.shape[0]
    decay = [jnp.exp(-lam[m]) for m in range(order)]

    def body(t, state):
        for u in range(unroll):
            state = tuple(decay[m] * state[m] for m in range(order))
            y_ref[t * unroll + u] = y_ref[t * unroll + u] + tree_sum(state)
        return state

    lax.fori_loop(0, y_ref.shape[0] // unroll, body, start)


def gate_out(dst, q_ref, k_ref, v_ref, skip_ref, y_ref):
    for j in range(q_ref.shape[1] // LANES):
        cols = pl.ds(j * LANES, LANES)
        gated_in = (k_ref[:, cols].astype(F32) * v_ref[:, cols].astype(F32)).astype(BF16)
        conv = y_ref[:, j, :].astype(BF16).astype(F32)
        total = conv + skip_ref[:, cols] * gated_in.astype(F32)
        dst[:, cols] = (q_ref[:, cols].astype(F32) * total).astype(BF16)


def flip(number, bits):
    for b in range(bits.bit_length()):
        if bits >> b & 1:
            number = number + (1 << b) - 2 * (1 << b) * (number // (1 << b) % 2)
    return number


def fused_kernel(
    n, tp, q_hbm, k_hbm, v_hbm, res_hbm, rate_hbm, skip_hbm, w_hbm, out_ref,
    q_ref, k_ref, v_ref, res_ref, rate_ref, skip_ref, w_ref,
    x_ref, lam, res, s_own, s_in, s_give, s_got, gated, share, cols_in, sums_in, from_low, from_high,
    load, s_send, s_recv, c_send, c_recv, g_send, g_recv, f_send, h_send, h_recv,
    p_send, p_recv, z_send, z_recv, hop_send, low_recv, high_recv,
):
    me = lax.axis_index("ctx")
    row = lax.axis_index("tp")
    core = me % 2
    chip = me // 2
    sib = me + 1 - 2 * core
    chips = n // 2
    per_tp = n // tp
    tok = q_ref.shape[0]
    half = tok // 2
    order = lam.shape[0]
    shape = lam.shape[1:]

    pairs = (
        (k_hbm, k_ref), (v_hbm, v_ref), (rate_hbm, rate_ref), (res_hbm, res_ref),
        (q_hbm, q_ref), (skip_hbm, skip_ref), (w_hbm, w_ref),
    )
    loads = [pltpu.make_async_copy(src, dst, load.at[i]) for i, (src, dst) in enumerate(pairs)]
    for copy in loads:
        copy.start()

    barrier = pltpu.get_barrier_semaphore()
    for d in range(1, n):
        pl.semaphore_signal(barrier, inc=1, device_id={"ctx": (me + d) % n}, device_id_type=MESH)

    for d in range(1, tp):
        pl.semaphore_signal(barrier, inc=1, device_id={"tp": (row + d) % tp}, device_id_type=MESH)

    for copy in loads[:3]:
        copy.wait()
    spread_channels(x_ref, gate_in(k_ref, v_ref).astype(F32))
    spread_channels(lam, rate_ref[...])
    zero = tuple(jnp.zeros(shape, F32) for _ in range(order))
    state = run_states(x_ref, lam, zero)
    for m in range(order):
        s_own[m] = state[m]

    pl.semaphore_wait(barrier, n - 1 + tp - 1)

    def over(axis, index, src, dst, send, recv):
        return pltpu.make_async_remote_copy(
            src_ref=src, dst_ref=dst, send_sem=send, recv_sem=recv,
            device_id={axis: index}, device_id_type=MESH,
        )

    def state_copy(d, slot):
        return over("ctx", flip(chip, d) * 2 + core, s_own, s_in.at[slot], s_send.at[d], s_recv.at[slot])

    for d in range(1, chips):
        state_copy(d, chip).start()
    loads[3].wait()
    spread_channels(res, res_ref[...])
    run_conv(x_ref, lam, res, zero)
    for copy in loads[4:]:
        copy.wait()
    for d in range(1, chips):
        state_copy(d, flip(chip, d)).wait_recv()

    def carry_for(target, dst):
        def weight(source):
            steps = (jnp.maximum(target - 1 - source, 0) * tok).astype(F32)
            live = jnp.where(source < target, 1.0, 0.0).astype(F32)
            return steps, live

        weights = [weight(me)] + [weight(flip(chip, d) * 2 + core) for d in range(1, chips)]
        for m in range(order):
            total = jnp.zeros(shape, F32)
            for d in range(chips):
                part = s_own[m] if d == 0 else s_in[flip(chip, d), m]
                total = total + jnp.exp(-lam[m] * weights[d][0]) * weights[d][1] * part
            dst[m] = total

    carry_for(sib, s_give)
    carry_copy = over("ctx", sib, s_give, s_got, c_send, c_recv)
    carry_copy.start()
    carry_for(me, s_in.at[chip])
    carry_copy.wait_recv()
    add_carry(x_ref, lam, tuple(res[m] * (s_in[chip, m] + s_got[m]) for m in range(order)))
    gate_out(gated.at[me], q_ref, k_ref, v_ref, skip_ref, x_ref)

    def same_core(d):
        return flip(chip, d) * 2 + core

    def other_core(d):
        return flip(chip, d) * 2 + 1 - core

    def gated_copy(index, slot, send):
        return over("ctx", index, gated.at[slot], gated.at[slot], send, g_recv.at[slot])

    def half_copy(index, slot, part):
        rows = pl.ds(part * half, half)
        return over(
            "ctx", index, gated.at[slot, rows], gated.at[slot, rows], h_send.at[part], h_recv.at[part]
        )

    def product(i):
        return jnp.dot(gated[i], w_ref[...], preferred_element_type=F32).astype(BF16)

    def back_copy(i, slot):
        return over("ctx", i, share.at[i], cols_in.at[slot], p_send.at[i], p_recv.at[slot])

    def sum_copy(k, source):
        return over(
            "tp", k // per_tp, cols_in.at[k], sums_in.at[source, k % per_tp],
            z_send.at[k], z_recv.at[source, k % per_tp],
        )

    def low_copy(k, part):
        rows = pl.ds(part * half, half)
        return over(
            "tp", (row + tp - 1) % tp, cols_in.at[k, rows], from_high.at[k, rows],
            hop_send.at[k, part], high_recv.at[k, part],
        )

    def high_copy(k, part):
        rows = pl.ds(part * half, half)
        return over(
            "tp", (row + 1) % tp, cols_in.at[k, rows], from_low.at[k, rows],
            hop_send.at[k, part], low_recv.at[k, part],
        )

    def send_back(i):
        share[i] = product(i)
        back_copy(i, me).start()

    def send_on(k):
        @pl.when(k // per_tp != row)
        def _():
            sum_copy(k, row).start()

    def hop(k):
        back_copy(k, k).wait_recv()
        target = k // per_tp
        for part in range(2):
            rows = pl.ds(part * half, half)

            @pl.when(row > target)
            def _():
                @pl.when(row < tp - 1)
                def _():
                    low_copy(k, part).wait_recv()
                    both = cols_in[k, rows].astype(F32) + from_high[k, rows].astype(F32)
                    cols_in[k, rows] = both.astype(BF16)

                low_copy(k, part).start()

            @pl.when(row < target)
            def _():
                @pl.when(row > 0)
                def _():
                    high_copy(k, part).wait_recv()
                    both = cols_in[k, rows].astype(F32) + from_low[k, rows].astype(F32)
                    cols_in[k, rows] = both.astype(BF16)

                high_copy(k, part).start()

    def take_other(d):
        i = other_core(d)
        gated_copy(sib, i, f_send.at[d]).wait_recv()
        send_back(i)

    gated_copy(same_core(1), me, g_send.at[1]).start()
    gated_copy(same_core(2), me, g_send.at[2]).start()
    gated_copy(sib, me, g_send.at[0]).start()
    cols_in[me] = product(me)
    gated_copy(sib, sib, g_send.at[0]).wait_recv()
    send_back(sib)
    send_on(me)
    for d in (1, 2):
        i = same_core(d)
        gated_copy(i, i, g_send.at[d]).wait_recv()
        half_copy(same_core(3 - d), i, 2 - d).start()
        gated_copy(sib, i, f_send.at[d]).start()
        send_back(i)
    back_copy(sib, sib).wait_recv()
    send_on(sib)
    take_other(1)
    take_other(2)
    far = same_core(3)
    half_copy(me, far, 0).wait_recv()
    half_copy(me, far, 1).wait_recv()
    gated_copy(sib, far, f_send.at[3]).start()
    send_back(far)
    take_other(3)
    for d in range(1, chips):
        hop(same_core(d))
        hop(other_core(d))

    width = w_ref.shape[1]
    for h in range(per_tp):
        k = row * per_tp + h
        cols = pl.ds(h * width, width)

        @pl.when(row == chip)
        def _():
            total = cols_in[k].astype(F32)
            for d in range(1, tp):
                source = (row + d) % tp
                sum_copy(k, source).wait_recv()
                total = total + sums_in[source, h].astype(F32)
            out_ref[:, cols] = total.astype(BF16)

        @pl.when(row != chip)
        def _():
            for part in range(2):
                rows = pl.ds(part * half, half)

                @pl.when(row == 0)
                def _():
                    low_copy(k, part).wait_recv()
                    both = cols_in[k, rows].astype(F32) + from_high[k, rows].astype(F32)
                    out_ref[rows, cols] = both.astype(BF16)

                @pl.when(row == tp - 1)
                def _():
                    high_copy(k, part).wait_recv()
                    both = cols_in[k, rows].astype(F32) + from_low[k, rows].astype(F32)
                    out_ref[rows, cols] = both.astype(BF16)

                @pl.when((row > 0) & (row < tp - 1))
                def _():
                    low_copy(k, part).wait_recv()
                    high_copy(k, part).wait_recv()
                    both = from_low[k, rows].astype(F32) + from_high[k, rows].astype(F32)
                    out_ref[rows, cols] = (cols_in[k, rows].astype(F32) + both).astype(BF16)

    carry_copy.wait_send()
    gated_copy(sib, me, g_send.at[0]).wait_send()
    for d in range(1, chips):
        state_copy(d, chip).wait_send()
        gated_copy(sib, same_core(d), f_send.at[d]).wait_send()
    for d in (1, 2):
        gated_copy(same_core(d), me, g_send.at[d]).wait_send()
        half_copy(same_core(3 - d), same_core(d), 2 - d).wait_send()
    for d in range(1, n):
        back_copy((me + d) % n, me).wait_send()
    for k in range(n):
        own = k // per_tp == chip

        @pl.when((k // per_tp != row) & own)
        def _():
            sum_copy(k, row).wait_send()

        @pl.when((k // per_tp != row) & jnp.logical_not(own))
        def _():
            for part in range(2):
                low_copy(k, part).wait_send()


def fused(n, tp, query, keys, values, residues, rates, skip_gain, w_out):
    tok, chans = query.shape
    order = residues.shape[1]
    width = w_out.shape[1]
    per_tp = n // tp
    poles = (order, chans // LANES, LANES)
    dma = pltpu.SemaphoreType.DMA
    vmem = pltpu.VMEM
    blocks = vmem((n, tok, width), BF16)
    return pl.pallas_call(
        functools.partial(fused_kernel, n, tp),
        out_shape=jax.ShapeDtypeStruct((tok, per_tp * width), BF16),
        in_specs=[pl.BlockSpec(memory_space=pltpu.HBM)] * 7,
        out_specs=pl.BlockSpec(memory_space=pltpu.VMEM),
        scratch_shapes=[
            vmem((tok, chans), BF16), vmem((tok, chans), BF16), vmem((tok, chans), BF16),
            vmem((order, chans), F32), vmem((order, chans), F32), vmem((1, chans), F32),
            vmem((chans, width), BF16),
            vmem((tok,) + poles[1:], F32),
            vmem(poles, F32), vmem(poles, F32), vmem(poles, F32),
            vmem((n // 2,) + poles, F32), vmem(poles, F32), vmem(poles, F32),
            vmem((n, tok, chans), BF16),
            blocks, blocks, vmem((tp, per_tp, tok, width), BF16), blocks, blocks,
            dma((7,)), dma((n // 2,)), dma((n // 2,)), dma, dma, dma((3,)), dma((n,)), dma((n // 2,)),
            dma((2,)), dma((2,)), dma((n,)), dma((n,)), dma((n,)), dma((tp, per_tp)), dma((n, 2)), dma((n, 2)), dma((n, 2)),
        ],
        compiler_params=pltpu.CompilerParams(
            collective_id=0, has_side_effects=True, vmem_limit_bytes=60 * 2**20
        ),
    )(query, keys, values, residues.T, rates.T, skip_gain[None, :], w_out)


def states_kernel(k_ref, v_ref, rate_ref, s_ref, x_ref, lam):
    spread_channels(x_ref, gate_in(k_ref, v_ref).astype(F32))
    spread_channels(lam, rate_ref[...])
    zero = tuple(jnp.zeros(lam.shape[1:], F32) for _ in range(lam.shape[0]))
    state = run_states(x_ref, lam, zero)
    for m in range(lam.shape[0]):
        s_ref[m] = state[m]


def conv_kernel(q_ref, k_ref, v_ref, res_ref, rate_ref, skip_ref, s_ref, out_ref, x_ref, lam, res):
    spread_channels(x_ref, gate_in(k_ref, v_ref).astype(F32))
    spread_channels(lam, rate_ref[...])
    spread_channels(res, res_ref[...])
    run_conv(x_ref, lam, res, tuple(s_ref[m] for m in range(lam.shape[0])))
    gate_out(out_ref, q_ref, k_ref, v_ref, skip_ref, x_ref)


def gathered(n, query, keys, values, residues, rates, skip_gain, w_out):
    tok, chans = query.shape
    order = residues.shape[1]
    poles = (order, chans // LANES, LANES)
    block = (tok,) + poles[1:]
    vmem = pl.BlockSpec(memory_space=pltpu.VMEM)
    state = pl.pallas_call(
        states_kernel,
        out_shape=jax.ShapeDtypeStruct(poles, F32),
        in_specs=[vmem] * 3,
        out_specs=vmem,
        scratch_shapes=[pltpu.VMEM(block, F32), pltpu.VMEM(poles, F32)],
        compiler_params=pltpu.CompilerParams(vmem_limit_bytes=24 * 2**20),
    )(keys, values, rates.T)
    me = lax.axis_index("ctx")
    lam = rates.T.reshape(poles)
    blocks = lax.all_gather(state, "ctx")
    away = me - 1 - jnp.arange(n, dtype=jnp.int32)
    steps = (jnp.maximum(away, 0) * tok).astype(F32)[:, None, None, None]
    live = (away >= 0)[:, None, None, None]
    carry = jnp.sum(jnp.where(live, jnp.exp(-lam[None] * steps) * blocks, 0.0), axis=0)
    gated = pl.pallas_call(
        conv_kernel,
        out_shape=jax.ShapeDtypeStruct((tok, chans), BF16),
        in_specs=[vmem] * 7,
        out_specs=vmem,
        scratch_shapes=[pltpu.VMEM(block, F32), pltpu.VMEM(poles, F32), pltpu.VMEM(poles, F32)],
        compiler_params=pltpu.CompilerParams(vmem_limit_bytes=24 * 2**20),
    )(query, keys, values, residues.T, rates.T, skip_gain[None, :], carry)
    weights = lax.all_gather(w_out, "ctx", axis=1, tiled=True)
    part = jnp.dot(gated, weights, preferred_element_type=F32).astype(BF16)
    return lax.psum_scatter(part, "tp", scatter_dimension=1, tiled=True)


def solution(mesh):
    n, tp = mesh.shape["ctx"], mesh.shape["tp"]

    def per_device(query, keys, values, residues, rates, skip_gain, w_out):
        args = (query, keys, values, residues, rates, skip_gain, w_out)
        few_tokens = n * query.shape[0] <= tp * query.shape[1]
        even = n == 8 and n == 2 * tp and w_out.shape[1] % LANES == 0
        if few_tokens and even:
            return fused(n, tp, *args)
        return gathered(n, *args)

    placed = (
        P("ctx", "tp"),
        P("ctx", "tp"),
        P("ctx", "tp"),
        P("tp", None),
        P("tp", None),
        P("tp"),
        P("tp", "ctx"),
    )
    return jax.shard_map(
        per_device, mesh=mesh, in_specs=placed, out_specs=P("ctx", "tp"), check_vma=False
    )
```

```python
import functools

import jax
import jax.numpy as jnp
from jax import lax
from jax.experimental import pallas as pl
from jax.experimental.pallas import tpu as pltpu
from jax.sharding import PartitionSpec as P

MESH = pl.DeviceIdType.MESH
LANES = 128
F32 = jnp.float32
BF16 = jnp.bfloat16


def spread_channels(dst, value):
    for j in range(value.shape[1] // LANES):
        dst[:, j, :] = value[:, j * LANES : (j + 1) * LANES]


def gate_in(keys, values):
    return (keys[...].astype(F32) * values[...].astype(F32)).astype(BF16)


def tree_sum(terms):
    terms = list(terms)
    while len(terms) > 1:
        odd = [terms[-1]] if len(terms) % 2 else []
        terms = [terms[i] + terms[i + 1] for i in range(0, len(terms) - 1, 2)] + odd
    return terms[0]


def run_states(x_ref, lam, start, unroll=8):
    order = lam.shape[0]
    decay = [jnp.exp(-lam[m]) for m in range(order)]

    def body(t, state):
        for u in range(unroll):
            token = x_ref[t * unroll + u]
            state = tuple(decay[m] * state[m] + token for m in range(order))
        return state

    return lax.fori_loop(0, x_ref.shape[0] // unroll, body, start)


def run_conv(x_ref, lam, res, start, unroll=4):
    order = lam.shape[0]
    decay = [jnp.exp(-lam[m]) for m in range(order)]

    def body(t, state):
        for u in range(unroll):
            token = x_ref[t * unroll + u]
            state = tuple(decay[m] * state[m] + token for m in range(order))
            x_ref[t * unroll + u] = tree_sum([res[m] * state[m] for m in range(order)])
        return state

    lax.fori_loop(0, x_ref.shape[0] // unroll, body, start)


def add_carry(y_ref, lam, start, unroll=8):
    order = lam.shape[0]
    decay = [jnp.exp(-lam[m]) for m in range(order)]

    def body(t, state):
        for u in range(unroll):
            state = tuple(decay[m] * state[m] for m in range(order))
            y_ref[t * unroll + u] = y_ref[t * unroll + u] + tree_sum(state)
        return state

    lax.fori_loop(0, y_ref.shape[0] // unroll, body, start)


def gate_out(dst, q_ref, k_ref, v_ref, skip_ref, y_ref):
    for j in range(q_ref.shape[1] // LANES):
        cols = pl.ds(j * LANES, LANES)
        gated_in = (k_ref[:, cols].astype(F32) * v_ref[:, cols].astype(F32)).astype(BF16)
        conv = y_ref[:, j, :].astype(BF16).astype(F32)
        total = conv + skip_ref[:, cols] * gated_in.astype(F32)
        dst[:, cols] = (q_ref[:, cols].astype(F32) * total).astype(BF16)


def flip(number, bits):
    for b in range(bits.bit_length()):
        if bits >> b & 1:
            number = number + (1 << b) - 2 * (1 << b) * (number // (1 << b) % 2)
    return number


def fused_kernel(
    n, tp, q_hbm, k_hbm, v_hbm, res_hbm, rate_hbm, skip_hbm, w_hbm, out_ref,
    q_ref, k_ref, v_ref, res_ref, rate_ref, skip_ref, w_ref,
    x_ref, lam, res, s_own, s_in, s_give, s_got, gated, share, cols_in, sums_in,
    load, s_send, s_recv, c_send, c_recv, g_send, g_recv, f_send, h_send, h_recv,
    p_send, p_recv, z_send, z_recv,
):
    me = lax.axis_index("ctx")
    row = lax.axis_index("tp")
    core = me % 2
    chip = me // 2
    sib = me + 1 - 2 * core
    chips = n // 2
    per_tp = n // tp
    tok = q_ref.shape[0]
    half = tok // 2
    quarter = tok // 4
    order = lam.shape[0]
    shape = lam.shape[1:]

    pairs = (
        (k_hbm, k_ref), (v_hbm, v_ref), (rate_hbm, rate_ref), (res_hbm, res_ref),
        (q_hbm, q_ref), (skip_hbm, skip_ref), (w_hbm, w_ref),
    )
    loads = [pltpu.make_async_copy(src, dst, load.at[i]) for i, (src, dst) in enumerate(pairs)]
    for copy in loads:
        copy.start()

    barrier = pltpu.get_barrier_semaphore()
    for d in range(1, n):
        pl.semaphore_signal(barrier, inc=1, device_id={"ctx": (me + d) % n}, device_id_type=MESH)

    for d in range(1, tp):
        pl.semaphore_signal(barrier, inc=1, device_id={"tp": (row + d) % tp}, device_id_type=MESH)

    for copy in loads[:3]:
        copy.wait()
    spread_channels(x_ref, gate_in(k_ref, v_ref).astype(F32))
    spread_channels(lam, rate_ref[...])
    zero = tuple(jnp.zeros(shape, F32) for _ in range(order))
    state = run_states(x_ref, lam, zero)
    for m in range(order):
        s_own[m] = state[m]

    pl.semaphore_wait(barrier, n - 1 + tp - 1)

    def over(axis, index, src, dst, send, recv):
        return pltpu.make_async_remote_copy(
            src_ref=src, dst_ref=dst, send_sem=send, recv_sem=recv,
            device_id={axis: index}, device_id_type=MESH,
        )

    def state_copy(d, slot):
        return over("ctx", flip(chip, d) * 2 + core, s_own, s_in.at[slot], s_send.at[d], s_recv.at[slot])

    for d in range(1, chips):
        state_copy(d, chip).start()
    loads[3].wait()
    spread_channels(res, res_ref[...])
    run_conv(x_ref, lam, res, zero)
    for copy in loads[4:]:
        copy.wait()
    for d in range(1, chips):
        state_copy(d, flip(chip, d)).wait_recv()

    def carry_for(target, dst):
        def weight(source):
            steps = (jnp.maximum(target - 1 - source, 0) * tok).astype(F32)
            live = jnp.where(source < target, 1.0, 0.0).astype(F32)
            return steps, live

        weights = [weight(me)] + [weight(flip(chip, d) * 2 + core) for d in range(1, chips)]
        for m in range(order):
            total = jnp.zeros(shape, F32)
            for d in range(chips):
                part = s_own[m] if d == 0 else s_in[flip(chip, d), m]
                total = total + jnp.exp(-lam[m] * weights[d][0]) * weights[d][1] * part
            dst[m] = total

    carry_for(sib, s_give)
    carry_copy = over("ctx", sib, s_give, s_got, c_send, c_recv)
    carry_copy.start()
    carry_for(me, s_in.at[chip])
    carry_copy.wait_recv()
    add_carry(x_ref, lam, tuple(res[m] * (s_in[chip, m] + s_got[m]) for m in range(order)))
    gate_out(gated.at[me], q_ref, k_ref, v_ref, skip_ref, x_ref)

    def same_core(d):
        return flip(chip, d) * 2 + core

    def other_core(d):
        return flip(chip, d) * 2 + 1 - core

    def part_of(e):
        return pl.ds(e * half, half)

    def gated_copy(index, slot, e, send):
        block = gated.at[slot, part_of(e)]
        return over("ctx", index, block, block, send, g_recv.at[slot, e])

    def first_copy(d, e):
        return gated_copy(sib if d == 0 else same_core(d), me, e, g_send.at[d, e])

    def forward_copy(d, e):
        return gated_copy(sib, same_core(d), e, f_send.at[d, e])

    def relay_copy(index, slot, e, part):
        block = gated.at[slot, pl.ds(e * half + part * quarter, quarter)]
        return over("ctx", index, block, block, h_send.at[e, part], h_recv.at[e, part])

    def product(i, e):
        return jnp.dot(gated[i, part_of(e)], w_ref[...], preferred_element_type=F32).astype(BF16)

    def back_copy(i, slot, e):
        return over(
            "ctx", i, share.at[i, part_of(e)], cols_in.at[slot, part_of(e)],
            p_send.at[i, e], p_recv.at[slot, e],
        )

    def sum_copy(k, source, e):
        return over(
            "tp", k // per_tp, cols_in.at[k, part_of(e)], sums_in.at[source, k % per_tp, part_of(e)],
            z_send.at[k, e], z_recv.at[source, k % per_tp, e],
        )

    def send_back(i, e):
        share[i, part_of(e)] = product(i, e)
        back_copy(i, me, e).start()

    def send_on(k, e):
        @pl.when(k // per_tp != row)
        def _():
            sum_copy(k, row, e).start()

    def arrived(k, e):
        back_copy(k, k, e).wait_recv()
        send_on(k, e)

    def take_sib(e):
        gated_copy(sib, sib, e, g_send.at[0, e]).wait_recv()
        send_back(sib, e)

    def take_same(d, e):
        i = same_core(d)
        gated_copy(i, i, e, g_send.at[d, e]).wait_recv()
        relay_copy(same_core(3 - d), i, e, 2 - d).start()
        forward_copy(d, e).start()
        send_back(i, e)

    def take_far(e):
        i = same_core(3)
        relay_copy(me, i, e, 0).wait_recv()
        relay_copy(me, i, e, 1).wait_recv()
        forward_copy(3, e).start()
        send_back(i, e)

    def take_other(d, e):
        i = other_core(d)
        gated_copy(sib, i, e, f_send.at[d, e]).wait_recv()
        send_back(i, e)

    def send_first(e):
        first_copy(1, e).start()
        first_copy(2, e).start()
        first_copy(0, e).start()
        cols_in[me, part_of(e)] = product(me, e)
        send_on(me, e)

    send_first(0)
    take_sib(0)
    for d in range(chips - 1):
        first_copy(d, 0).wait_send()
    send_first(1)
    take_same(1, 0)
    take_same(2, 0)
    arrived(sib, 0)
    take_sib(1)
    take_other(1, 0)
    take_other(2, 0)
    take_far(0)
    arrived(same_core(1), 0)
    arrived(same_core(2), 0)
    take_same(1, 1)
    take_same(2, 1)
    take_other(3, 0)
    arrived(other_core(1), 0)
    arrived(other_core(2), 0)
    arrived(sib, 1)
    take_other(1, 1)
    take_other(2, 1)
    take_far(1)
    arrived(same_core(3), 0)
    arrived(other_core(3), 0)
    take_other(3, 1)
    for d in range(1, chips):
        arrived(same_core(d), 1)
        arrived(other_core(d), 1)

    width = w_ref.shape[1]
    for e in range(2):
        for h in range(per_tp):
            total = cols_in[row * per_tp + h, part_of(e)].astype(F32)
            for d in range(1, tp):
                source = (row + d) % tp
                sum_copy(row * per_tp + h, source, e).wait_recv()
                total = total + sums_in[source, h, part_of(e)].astype(F32)
            out_ref[part_of(e), pl.ds(h * width, width)] = total.astype(BF16)

    carry_copy.wait_send()
    for d in range(1, chips):
        state_copy(d, chip).wait_send()
    for d in range(chips - 1):
        first_copy(d, 1).wait_send()
    for e in range(2):
        for d in range(1, chips):
            forward_copy(d, e).wait_send()
        for d in (1, 2):
            relay_copy(same_core(3 - d), same_core(d), e, 2 - d).wait_send()
        for d in range(1, n):
            back_copy((me + d) % n, me, e).wait_send()
        for k in range(n):
            @pl.when(k // per_tp != row)
            def _():
                sum_copy(k, row, e).wait_send()


def fused(n, tp, query, keys, values, residues, rates, skip_gain, w_out):
    tok, chans = query.shape
    order = residues.shape[1]
    width = w_out.shape[1]
    per_tp = n // tp
    poles = (order, chans // LANES, LANES)
    dma = pltpu.SemaphoreType.DMA
    vmem = pltpu.VMEM
    blocks = vmem((n, tok, width), BF16)
    return pl.pallas_call(
        functools.partial(fused_kernel, n, tp),
        out_shape=jax.ShapeDtypeStruct((tok, per_tp * width), BF16),
        in_specs=[pl.BlockSpec(memory_space=pltpu.HBM)] * 7,
        out_specs=pl.BlockSpec(memory_space=pltpu.VMEM),
        scratch_shapes=[
            vmem((tok, chans), BF16), vmem((tok, chans), BF16), vmem((tok, chans), BF16),
            vmem((order, chans), F32), vmem((order, chans), F32), vmem((1, chans), F32),
            vmem((chans, width), BF16),
            vmem((tok,) + poles[1:], F32),
            vmem(poles, F32), vmem(poles, F32), vmem(poles, F32),
            vmem((n // 2,) + poles, F32), vmem(poles, F32), vmem(poles, F32),
            vmem((n, tok, chans), BF16),
            blocks, blocks, vmem((tp, per_tp, tok, width), BF16),
            dma((7,)), dma((n // 2,)), dma((n // 2,)), dma, dma, dma((3, 2)), dma((n, 2)), dma((n // 2, 2)),
            dma((2, 2)), dma((2, 2)), dma((n, 2)), dma((n, 2)), dma((n, 2)), dma((tp, per_tp, 2)),
        ],
        compiler_params=pltpu.CompilerParams(
            collective_id=0, has_side_effects=True, vmem_limit_bytes=60 * 2**20
        ),
    )(query, keys, values, residues.T, rates.T, skip_gain[None, :], w_out)


def states_kernel(k_ref, v_ref, rate_ref, s_ref, x_ref, lam):
    spread_channels(x_ref, gate_in(k_ref, v_ref).astype(F32))
    spread_channels(lam, rate_ref[...])
    zero = tuple(jnp.zeros(lam.shape[1:], F32) for _ in range(lam.shape[0]))
    state = run_states(x_ref, lam, zero)
    for m in range(lam.shape[0]):
        s_ref[m] = state[m]


def conv_kernel(q_ref, k_ref, v_ref, res_ref, rate_ref, skip_ref, s_ref, out_ref, x_ref, lam, res):
    spread_channels(x_ref, gate_in(k_ref, v_ref).astype(F32))
    spread_channels(lam, rate_ref[...])
    spread_channels(res, res_ref[...])
    run_conv(x_ref, lam, res, tuple(s_ref[m] for m in range(lam.shape[0])))
    gate_out(out_ref, q_ref, k_ref, v_ref, skip_ref, x_ref)


def gathered(n, query, keys, values, residues, rates, skip_gain, w_out):
    tok, chans = query.shape
    order = residues.shape[1]
    poles = (order, chans // LANES, LANES)
    block = (tok,) + poles[1:]
    vmem = pl.BlockSpec(memory_space=pltpu.VMEM)
    state = pl.pallas_call(
        states_kernel,
        out_shape=jax.ShapeDtypeStruct(poles, F32),
        in_specs=[vmem] * 3,
        out_specs=vmem,
        scratch_shapes=[pltpu.VMEM(block, F32), pltpu.VMEM(poles, F32)],
        compiler_params=pltpu.CompilerParams(vmem_limit_bytes=24 * 2**20),
    )(keys, values, rates.T)
    me = lax.axis_index("ctx")
    lam = rates.T.reshape(poles)
    blocks = lax.all_gather(state, "ctx")
    away = me - 1 - jnp.arange(n, dtype=jnp.int32)
    steps = (jnp.maximum(away, 0) * tok).astype(F32)[:, None, None, None]
    live = (away >= 0)[:, None, None, None]
    carry = jnp.sum(jnp.where(live, jnp.exp(-lam[None] * steps) * blocks, 0.0), axis=0)
    gated = pl.pallas_call(
        conv_kernel,
        out_shape=jax.ShapeDtypeStruct((tok, chans), BF16),
        in_specs=[vmem] * 7,
        out_specs=vmem,
        scratch_shapes=[pltpu.VMEM(block, F32), pltpu.VMEM(poles, F32), pltpu.VMEM(poles, F32)],
        compiler_params=pltpu.CompilerParams(vmem_limit_bytes=24 * 2**20),
    )(query, keys, values, residues.T, rates.T, skip_gain[None, :], carry)
    weights = lax.all_gather(w_out, "ctx", axis=1, tiled=True)
    part = jnp.dot(gated, weights, preferred_element_type=F32).astype(BF16)
    return lax.psum_scatter(part, "tp", scatter_dimension=1, tiled=True)


def solution(mesh):
    n, tp = mesh.shape["ctx"], mesh.shape["tp"]

    def per_device(query, keys, values, residues, rates, skip_gain, w_out):
        args = (query, keys, values, residues, rates, skip_gain, w_out)
        few_tokens = n * query.shape[0] <= tp * query.shape[1]
        even = n == 8 and n % tp == 0 and w_out.shape[1] % LANES == 0 and query.shape[0] % 64 == 0
        if few_tokens and even:
            return fused(n, tp, *args)
        return gathered(n, *args)

    placed = (
        P("ctx", "tp"),
        P("ctx", "tp"),
        P("ctx", "tp"),
        P("tp", None),
        P("tp", None),
        P("tp"),
        P("tp", "ctx"),
    )
    return jax.shard_map(
        per_device, mesh=mesh, in_specs=placed, out_specs=P("ctx", "tp"), check_vma=False
    )
```

```python
import functools

import jax
import jax.numpy as jnp
from jax import lax
from jax.experimental import pallas as pl
from jax.experimental.pallas import tpu as pltpu
from jax.sharding import PartitionSpec as P

MESH = pl.DeviceIdType.MESH
LANES = 128
F32 = jnp.float32
BF16 = jnp.bfloat16


def spread_channels(dst, value):
    for j in range(value.shape[1] // LANES):
        dst[:, j, :] = value[:, j * LANES : (j + 1) * LANES]


def gate_in(keys, values):
    return (keys[...].astype(F32) * values[...].astype(F32)).astype(BF16)


def tree_sum(terms):
    terms = list(terms)
    while len(terms) > 1:
        odd = [terms[-1]] if len(terms) % 2 else []
        terms = [terms[i] + terms[i + 1] for i in range(0, len(terms) - 1, 2)] + odd
    return terms[0]


def run_states(x_ref, lam, start, unroll=8):
    order = lam.shape[0]
    decay = [jnp.exp(-lam[m]) for m in range(order)]

    def body(t, state):
        for u in range(unroll):
            token = x_ref[t * unroll + u]
            state = tuple(decay[m] * state[m] + token for m in range(order))
        return state

    return lax.fori_loop(0, x_ref.shape[0] // unroll, body, start)


def run_conv(x_ref, lam, res, start, unroll=4):
    order = lam.shape[0]
    decay = [jnp.exp(-lam[m]) for m in range(order)]

    def body(t, state):
        for u in range(unroll):
            token = x_ref[t * unroll + u]
            state = tuple(decay[m] * state[m] + token for m in range(order))
            x_ref[t * unroll + u] = tree_sum([res[m] * state[m] for m in range(order)])
        return state

    lax.fori_loop(0, x_ref.shape[0] // unroll, body, start)


def add_carry(y_ref, lam, start, unroll=8):
    order = lam.shape[0]
    decay = [jnp.exp(-lam[m]) for m in range(order)]

    def body(t, state):
        for u in range(unroll):
            state = tuple(decay[m] * state[m] for m in range(order))
            y_ref[t * unroll + u] = y_ref[t * unroll + u] + tree_sum(state)
        return state

    lax.fori_loop(0, y_ref.shape[0] // unroll, body, start)


def gate_out(dst, q_ref, k_ref, v_ref, skip_ref, y_ref):
    for j in range(q_ref.shape[1] // LANES):
        cols = pl.ds(j * LANES, LANES)
        gated_in = (k_ref[:, cols].astype(F32) * v_ref[:, cols].astype(F32)).astype(BF16)
        conv = y_ref[:, j, :].astype(BF16).astype(F32)
        total = conv + skip_ref[:, cols] * gated_in.astype(F32)
        dst[:, cols] = (q_ref[:, cols].astype(F32) * total).astype(BF16)


def flip(number, bits):
    for b in range(bits.bit_length()):
        if bits >> b & 1:
            number = number + (1 << b) - 2 * (1 << b) * (number // (1 << b) % 2)
    return number


def fused_kernel(
    n, tp, q_hbm, k_hbm, v_hbm, res_hbm, rate_hbm, skip_hbm, w_hbm, out_ref,
    q_ref, k_ref, v_ref, res_ref, rate_ref, skip_ref, w_ref,
    x_ref, lam, res, s_own, s_in, s_give, s_got, gated, share, cols_in, sums_in, from_low, from_high,
    load, s_send, s_recv, c_send, c_recv, g_send, g_recv, f_send, h_send, h_recv,
    p_send, p_recv, z_send, z_recv, hop_send, low_recv, high_recv,
):
    me = lax.axis_index("ctx")
    row = lax.axis_index("tp")
    core = me % 2
    chip = me // 2
    sib = me + 1 - 2 * core
    chips = n // 2
    per_tp = n // tp
    tok = q_ref.shape[0]
    half = tok // 2
    quarter = tok // 4
    order = lam.shape[0]
    shape = lam.shape[1:]

    pairs = (
        (k_hbm, k_ref), (v_hbm, v_ref), (rate_hbm, rate_ref), (res_hbm, res_ref),
        (q_hbm, q_ref), (skip_hbm, skip_ref), (w_hbm, w_ref),
    )
    loads = [pltpu.make_async_copy(src, dst, load.at[i]) for i, (src, dst) in enumerate(pairs)]
    for copy in loads:
        copy.start()

    barrier = pltpu.get_barrier_semaphore()
    for d in range(1, n):
        pl.semaphore_signal(barrier, inc=1, device_id={"ctx": (me + d) % n}, device_id_type=MESH)

    for d in range(1, tp):
        pl.semaphore_signal(barrier, inc=1, device_id={"tp": (row + d) % tp}, device_id_type=MESH)

    for copy in loads[:3]:
        copy.wait()
    spread_channels(x_ref, gate_in(k_ref, v_ref).astype(F32))
    spread_channels(lam, rate_ref[...])
    zero = tuple(jnp.zeros(shape, F32) for _ in range(order))
    state = run_states(x_ref, lam, zero)
    for m in range(order):
        s_own[m] = state[m]

    pl.semaphore_wait(barrier, n - 1 + tp - 1)

    def over(axis, index, src, dst, send, recv):
        return pltpu.make_async_remote_copy(
            src_ref=src, dst_ref=dst, send_sem=send, recv_sem=recv,
            device_id={axis: index}, device_id_type=MESH,
        )

    def state_copy(d, slot):
        return over("ctx", flip(chip, d) * 2 + core, s_own, s_in.at[slot], s_send.at[d], s_recv.at[slot])

    for d in range(1, chips):
        state_copy(d, chip).start()
    loads[3].wait()
    spread_channels(res, res_ref[...])
    run_conv(x_ref, lam, res, zero)
    for copy in loads[4:]:
        copy.wait()
    for d in range(1, chips):
        state_copy(d, flip(chip, d)).wait_recv()

    def carry_for(target, dst):
        def weight(source):
            steps = (jnp.maximum(target - 1 - source, 0) * tok).astype(F32)
            live = jnp.where(source < target, 1.0, 0.0).astype(F32)
            return steps, live

        weights = [weight(me)] + [weight(flip(chip, d) * 2 + core) for d in range(1, chips)]
        for m in range(order):
            total = jnp.zeros(shape, F32)
            for d in range(chips):
                part = s_own[m] if d == 0 else s_in[flip(chip, d), m]
                total = total + jnp.exp(-lam[m] * weights[d][0]) * weights[d][1] * part
            dst[m] = total

    carry_for(sib, s_give)
    carry_copy = over("ctx", sib, s_give, s_got, c_send, c_recv)
    carry_copy.start()
    carry_for(me, s_in.at[chip])
    carry_copy.wait_recv()
    add_carry(x_ref, lam, tuple(res[m] * (s_in[chip, m] + s_got[m]) for m in range(order)))
    gate_out(gated.at[me], q_ref, k_ref, v_ref, skip_ref, x_ref)

    def same_core(d):
        return flip(chip, d) * 2 + core

    def other_core(d):
        return flip(chip, d) * 2 + 1 - core

    def part_of(e):
        return pl.ds(e * half, half)

    def gated_copy(index, slot, e, send):
        block = gated.at[slot, part_of(e)]
        return over("ctx", index, block, block, send, g_recv.at[slot, e])

    def first_copy(d, e):
        return gated_copy(sib if d == 0 else same_core(d), me, e, g_send.at[d, e])

    def forward_copy(d, e):
        return gated_copy(sib, same_core(d), e, f_send.at[d, e])

    def relay_copy(index, slot, e, part):
        block = gated.at[slot, pl.ds(e * half + part * quarter, quarter)]
        return over("ctx", index, block, block, h_send.at[e, part], h_recv.at[e, part])

    def product(i, e):
        return jnp.dot(gated[i, part_of(e)], w_ref[...], preferred_element_type=F32).astype(BF16)

    def back_copy(i, slot, e):
        return over(
            "ctx", i, share.at[i, part_of(e)], cols_in.at[slot, part_of(e)],
            p_send.at[i, e], p_recv.at[slot, e],
        )

    def sum_copy(k, source, e):
        return over(
            "tp", k // per_tp, cols_in.at[k, part_of(e)], sums_in.at[source, k % per_tp, part_of(e)],
            z_send.at[k, e], z_recv.at[source, k % per_tp, e],
        )

    def low_copy(k, e):
        return over(
            "tp", (row + tp - 1) % tp, cols_in.at[k, part_of(e)], from_high.at[k % per_tp, part_of(e)],
            hop_send.at[k % per_tp, e], high_recv.at[k % per_tp, e],
        )

    def high_copy(k, e):
        return over(
            "tp", (row + 1) % tp, cols_in.at[k, part_of(e)], from_low.at[k % per_tp, part_of(e)],
            hop_send.at[k % per_tp, e], low_recv.at[k % per_tp, e],
        )

    def both(k, e, arrival):
        return cols_in[k, part_of(e)].astype(F32) + arrival[k % per_tp, part_of(e)].astype(F32)

    def hop(k, e):
        back_copy(k, k, e).wait_recv()
        target = k // per_tp

        @pl.when(row > target)
        def _():
            @pl.when(row < tp - 1)
            def _():
                low_copy(k, e).wait_recv()
                cols_in[k, part_of(e)] = both(k, e, from_high).astype(BF16)

            low_copy(k, e).start()

        @pl.when(row < target)
        def _():
            @pl.when(row > 0)
            def _():
                high_copy(k, e).wait_recv()
                cols_in[k, part_of(e)] = both(k, e, from_low).astype(BF16)

            high_copy(k, e).start()

    def send_back(i, e):
        share[i, part_of(e)] = product(i, e)
        back_copy(i, me, e).start()

    def send_on(k, e):
        @pl.when(k // per_tp != row)
        def _():
            sum_copy(k, row, e).start()

    def arrived(k, e):
        back_copy(k, k, e).wait_recv()
        send_on(k, e)

    def take_sib(e):
        gated_copy(sib, sib, e, g_send.at[0, e]).wait_recv()
        send_back(sib, e)

    def take_same(d, e):
        i = same_core(d)
        gated_copy(i, i, e, g_send.at[d, e]).wait_recv()
        relay_copy(same_core(3 - d), i, e, 2 - d).start()
        forward_copy(d, e).start()
        send_back(i, e)

    def take_far(e):
        i = same_core(3)
        relay_copy(me, i, e, 0).wait_recv()
        relay_copy(me, i, e, 1).wait_recv()
        forward_copy(3, e).start()
        send_back(i, e)

    def take_other(d, e):
        i = other_core(d)
        gated_copy(sib, i, e, f_send.at[d, e]).wait_recv()
        send_back(i, e)

    def send_first(e):
        first_copy(1, e).start()
        first_copy(2, e).start()
        first_copy(0, e).start()
        cols_in[me, part_of(e)] = product(me, e)
        send_on(me, e)

    send_first(0)
    take_sib(0)
    for d in range(chips - 1):
        first_copy(d, 0).wait_send()
    send_first(1)
    take_same(1, 0)
    take_same(2, 0)
    arrived(sib, 0)
    take_sib(1)
    take_other(1, 0)
    take_other(2, 0)
    take_far(0)
    arrived(same_core(1), 0)
    arrived(same_core(2), 0)
    take_same(1, 1)
    take_same(2, 1)
    take_other(3, 0)
    arrived(other_core(1), 0)
    arrived(other_core(2), 0)
    arrived(sib, 1)
    take_other(1, 1)
    take_other(2, 1)
    take_far(1)
    take_other(3, 1)
    for d in (1, 2):
        arrived(same_core(d), 1)
        arrived(other_core(d), 1)
    for e in range(2):
        hop(same_core(3), e)
        hop(other_core(3), e)

    width = w_ref.shape[1]
    last = flip(chip, 3)
    for e in range(2):
        for h in range(per_tp):
            k = row * per_tp + h
            cols = pl.ds(h * width, width)

            @pl.when(row != last)
            def _():
                total = cols_in[k, part_of(e)].astype(F32)
                for d in range(1, tp):
                    source = (row + d) % tp
                    sum_copy(k, source, e).wait_recv()
                    total = total + sums_in[source, h, part_of(e)].astype(F32)
                out_ref[part_of(e), cols] = total.astype(BF16)

            @pl.when((row == last) & (row == 0))
            def _():
                low_copy(k, e).wait_recv()
                out_ref[part_of(e), cols] = both(k, e, from_high).astype(BF16)

            @pl.when((row == last) & (row == tp - 1))
            def _():
                high_copy(k, e).wait_recv()
                out_ref[part_of(e), cols] = both(k, e, from_low).astype(BF16)

            @pl.when((row == last) & (row > 0) & (row < tp - 1))
            def _():
                low_copy(k, e).wait_recv()
                high_copy(k, e).wait_recv()
                total = both(k, e, from_low) + from_high[k % per_tp, part_of(e)].astype(F32)
                out_ref[part_of(e), cols] = total.astype(BF16)

    carry_copy.wait_send()
    for d in range(1, chips):
        state_copy(d, chip).wait_send()
    for d in range(chips - 1):
        first_copy(d, 1).wait_send()
    for e in range(2):
        for d in range(1, chips):
            forward_copy(d, e).wait_send()
        for d in (1, 2):
            relay_copy(same_core(3 - d), same_core(d), e, 2 - d).wait_send()
        for d in range(1, n):
            back_copy((me + d) % n, me, e).wait_send()
        for k in range(n):
            @pl.when((k // per_tp != row) & (k // per_tp != last))
            def _():
                sum_copy(k, row, e).wait_send()

            @pl.when((k // per_tp != row) & (k // per_tp == last))
            def _():
                low_copy(k, e).wait_send()


def fused(n, tp, query, keys, values, residues, rates, skip_gain, w_out):
    tok, chans = query.shape
    order = residues.shape[1]
    width = w_out.shape[1]
    per_tp = n // tp
    poles = (order, chans // LANES, LANES)
    dma = pltpu.SemaphoreType.DMA
    vmem = pltpu.VMEM
    blocks = vmem((n, tok, width), BF16)
    hops = vmem((per_tp, tok, width), BF16)
    return pl.pallas_call(
        functools.partial(fused_kernel, n, tp),
        out_shape=jax.ShapeDtypeStruct((tok, per_tp * width), BF16),
        in_specs=[pl.BlockSpec(memory_space=pltpu.HBM)] * 7,
        out_specs=pl.BlockSpec(memory_space=pltpu.VMEM),
        scratch_shapes=[
            vmem((tok, chans), BF16), vmem((tok, chans), BF16), vmem((tok, chans), BF16),
            vmem((order, chans), F32), vmem((order, chans), F32), vmem((1, chans), F32),
            vmem((chans, width), BF16),
            vmem((tok,) + poles[1:], F32),
            vmem(poles, F32), vmem(poles, F32), vmem(poles, F32),
            vmem((n // 2,) + poles, F32), vmem(poles, F32), vmem(poles, F32),
            vmem((n, tok, chans), BF16),
            blocks, blocks, vmem((tp, per_tp, tok, width), BF16), hops, hops,
            dma((7,)), dma((n // 2,)), dma((n // 2,)), dma, dma, dma((3, 2)), dma((n, 2)), dma((n // 2, 2)),
            dma((2, 2)), dma((2, 2)), dma((n, 2)), dma((n, 2)), dma((n, 2)), dma((tp, per_tp, 2)),
            dma((per_tp, 2)), dma((per_tp, 2)), dma((per_tp, 2)),
        ],
        compiler_params=pltpu.CompilerParams(
            collective_id=0, has_side_effects=True, vmem_limit_bytes=60 * 2**20
        ),
    )(query, keys, values, residues.T, rates.T, skip_gain[None, :], w_out)


def states_kernel(k_ref, v_ref, rate_ref, s_ref, x_ref, lam):
    spread_channels(x_ref, gate_in(k_ref, v_ref).astype(F32))
    spread_channels(lam, rate_ref[...])
    zero = tuple(jnp.zeros(lam.shape[1:], F32) for _ in range(lam.shape[0]))
    state = run_states(x_ref, lam, zero)
    for m in range(lam.shape[0]):
        s_ref[m] = state[m]


def conv_kernel(q_ref, k_ref, v_ref, res_ref, rate_ref, skip_ref, s_ref, out_ref, x_ref, lam, res):
    spread_channels(x_ref, gate_in(k_ref, v_ref).astype(F32))
    spread_channels(lam, rate_ref[...])
    spread_channels(res, res_ref[...])
    run_conv(x_ref, lam, res, tuple(s_ref[m] for m in range(lam.shape[0])))
    gate_out(out_ref, q_ref, k_ref, v_ref, skip_ref, x_ref)


def gathered(n, query, keys, values, residues, rates, skip_gain, w_out):
    tok, chans = query.shape
    order = residues.shape[1]
    poles = (order, chans // LANES, LANES)
    block = (tok,) + poles[1:]
    vmem = pl.BlockSpec(memory_space=pltpu.VMEM)
    state = pl.pallas_call(
        states_kernel,
        out_shape=jax.ShapeDtypeStruct(poles, F32),
        in_specs=[vmem] * 3,
        out_specs=vmem,
        scratch_shapes=[pltpu.VMEM(block, F32), pltpu.VMEM(poles, F32)],
        compiler_params=pltpu.CompilerParams(vmem_limit_bytes=24 * 2**20),
    )(keys, values, rates.T)
    me = lax.axis_index("ctx")
    lam = rates.T.reshape(poles)
    blocks = lax.all_gather(state, "ctx")
    away = me - 1 - jnp.arange(n, dtype=jnp.int32)
    steps = (jnp.maximum(away, 0) * tok).astype(F32)[:, None, None, None]
    live = (away >= 0)[:, None, None, None]
    carry = jnp.sum(jnp.where(live, jnp.exp(-lam[None] * steps) * blocks, 0.0), axis=0)
    gated = pl.pallas_call(
        conv_kernel,
        out_shape=jax.ShapeDtypeStruct((tok, chans), BF16),
        in_specs=[vmem] * 7,
        out_specs=vmem,
        scratch_shapes=[pltpu.VMEM(block, F32), pltpu.VMEM(poles, F32), pltpu.VMEM(poles, F32)],
        compiler_params=pltpu.CompilerParams(vmem_limit_bytes=24 * 2**20),
    )(query, keys, values, residues.T, rates.T, skip_gain[None, :], carry)
    weights = lax.all_gather(w_out, "ctx", axis=1, tiled=True)
    part = jnp.dot(gated, weights, preferred_element_type=F32).astype(BF16)
    return lax.psum_scatter(part, "tp", scatter_dimension=1, tiled=True)


def solution(mesh):
    n, tp = mesh.shape["ctx"], mesh.shape["tp"]

    def per_device(query, keys, values, residues, rates, skip_gain, w_out):
        args = (query, keys, values, residues, rates, skip_gain, w_out)
        few_tokens = n * query.shape[0] <= tp * query.shape[1]
        even = n == 8 and n == 2 * tp and w_out.shape[1] % LANES == 0 and query.shape[0] % 64 == 0
        if few_tokens and even:
            return fused(n, tp, *args)
        return gathered(n, *args)

    placed = (
        P("ctx", "tp"),
        P("ctx", "tp"),
        P("ctx", "tp"),
        P("tp", None),
        P("tp", None),
        P("tp"),
        P("tp", "ctx"),
    )
    return jax.shard_map(
        per_device, mesh=mesh, in_specs=placed, out_specs=P("ctx", "tp"), check_vma=False
    )
```

```python
import functools

import jax
import jax.numpy as jnp
from jax import lax
from jax.experimental import pallas as pl
from jax.experimental.pallas import tpu as pltpu
from jax.sharding import PartitionSpec as P

MESH = pl.DeviceIdType.MESH
LANES = 128
F32 = jnp.float32
BF16 = jnp.bfloat16


def spread_channels(dst, value):
    for j in range(value.shape[1] // LANES):
        dst[:, j, :] = value[:, j * LANES : (j + 1) * LANES]


def gate_in(keys, values):
    return (keys[...].astype(F32) * values[...].astype(F32)).astype(BF16)


def tree_sum(terms):
    terms = list(terms)
    while len(terms) > 1:
        odd = [terms[-1]] if len(terms) % 2 else []
        terms = [terms[i] + terms[i + 1] for i in range(0, len(terms) - 1, 2)] + odd
    return terms[0]


def run_states(x_ref, lam, start, unroll=8):
    order = lam.shape[0]
    decay = [jnp.exp(-lam[m]) for m in range(order)]

    def body(t, state):
        for u in range(unroll):
            token = x_ref[t * unroll + u]
            state = tuple(decay[m] * state[m] + token for m in range(order))
        return state

    return lax.fori_loop(0, x_ref.shape[0] // unroll, body, start)


def run_conv(x_ref, lam, res, start, unroll=4):
    order = lam.shape[0]
    decay = [jnp.exp(-lam[m]) for m in range(order)]

    def body(t, state):
        for u in range(unroll):
            token = x_ref[t * unroll + u]
            state = tuple(decay[m] * state[m] + token for m in range(order))
            x_ref[t * unroll + u] = tree_sum([res[m] * state[m] for m in range(order)])
        return state

    lax.fori_loop(0, x_ref.shape[0] // unroll, body, start)


def add_carry(y_ref, lam, start, unroll=8):
    order = lam.shape[0]
    decay = [jnp.exp(-lam[m]) for m in range(order)]

    def body(t, state):
        for u in range(unroll):
            state = tuple(decay[m] * state[m] for m in range(order))
            y_ref[t * unroll + u] = y_ref[t * unroll + u] + tree_sum(state)
        return state

    lax.fori_loop(0, y_ref.shape[0] // unroll, body, start)


def gate_out(dst, q_ref, k_ref, v_ref, skip_ref, y_ref):
    for j in range(q_ref.shape[1] // LANES):
        cols = pl.ds(j * LANES, LANES)
        gated_in = (k_ref[:, cols].astype(F32) * v_ref[:, cols].astype(F32)).astype(BF16)
        conv = y_ref[:, j, :].astype(BF16).astype(F32)
        total = conv + skip_ref[:, cols] * gated_in.astype(F32)
        dst[:, cols] = (q_ref[:, cols].astype(F32) * total).astype(BF16)


def flip(number, bits):
    for b in range(bits.bit_length()):
        if bits >> b & 1:
            number = number + (1 << b) - 2 * (1 << b) * (number // (1 << b) % 2)
    return number


def fused_kernel(
    n, tp, q_hbm, k_hbm, v_hbm, res_hbm, rate_hbm, skip_hbm, w_hbm, out_ref,
    q_ref, k_ref, v_ref, res_ref, rate_ref, skip_ref, w_ref,
    x_ref, lam, res, s_own, s_in, s_give, s_got, gated, share, cols_in, sums_in,
    load, s_send, s_recv, c_send, c_recv, g_send, g_recv, f_send, h_send, h_recv,
    p_send, p_recv, z_send, z_recv,
):
    me = lax.axis_index("ctx")
    row = lax.axis_index("tp")
    core = me % 2
    chip = me // 2
    sib = me + 1 - 2 * core
    chips = n // 2
    per_tp = n // tp
    tok = q_ref.shape[0]
    half = tok // 2
    quarter = tok // 4
    order = lam.shape[0]
    shape = lam.shape[1:]

    pairs = (
        (k_hbm, k_ref), (v_hbm, v_ref), (rate_hbm, rate_ref), (res_hbm, res_ref),
        (q_hbm, q_ref), (skip_hbm, skip_ref), (w_hbm, w_ref),
    )
    loads = [pltpu.make_async_copy(src, dst, load.at[i]) for i, (src, dst) in enumerate(pairs)]
    for copy in loads:
        copy.start()

    barrier = pltpu.get_barrier_semaphore()
    for d in range(1, n):
        pl.semaphore_signal(barrier, inc=1, device_id={"ctx": (me + d) % n}, device_id_type=MESH)

    for d in range(1, tp):
        pl.semaphore_signal(barrier, inc=1, device_id={"tp": (row + d) % tp}, device_id_type=MESH)

    for copy in loads[:3]:
        copy.wait()
    spread_channels(x_ref, gate_in(k_ref, v_ref).astype(F32))
    spread_channels(lam, rate_ref[...])
    zero = tuple(jnp.zeros(shape, F32) for _ in range(order))
    state = run_states(x_ref, lam, zero)
    for m in range(order):
        s_own[m] = state[m]

    pl.semaphore_wait(barrier, n - 1 + tp - 1)

    def over(axis, index, src, dst, send, recv):
        return pltpu.make_async_remote_copy(
            src_ref=src, dst_ref=dst, send_sem=send, recv_sem=recv,
            device_id={axis: index}, device_id_type=MESH,
        )

    def state_copy(d, slot):
        return over("ctx", flip(chip, d) * 2 + core, s_own, s_in.at[slot], s_send.at[d], s_recv.at[slot])

    for d in range(1, chips):
        state_copy(d, chip).start()
    loads[3].wait()
    spread_channels(res, res_ref[...])
    run_conv(x_ref, lam, res, zero)
    for copy in loads[4:]:
        copy.wait()
    for d in range(1, chips):
        state_copy(d, flip(chip, d)).wait_recv()

    def carry_for(target, dst):
        def weight(source):
            steps = (jnp.maximum(target - 1 - source, 0) * tok).astype(F32)
            live = jnp.where(source < target, 1.0, 0.0).astype(F32)
            return steps, live

        weights = [weight(me)] + [weight(flip(chip, d) * 2 + core) for d in range(1, chips)]
        for m in range(order):
            total = jnp.zeros(shape, F32)
            for d in range(chips):
                part = s_own[m] if d == 0 else s_in[flip(chip, d), m]
                total = total + jnp.exp(-lam[m] * weights[d][0]) * weights[d][1] * part
            dst[m] = total

    carry_for(sib, s_give)
    carry_copy = over("ctx", sib, s_give, s_got, c_send, c_recv)
    carry_copy.start()
    carry_for(me, s_in.at[chip])
    carry_copy.wait_recv()
    add_carry(x_ref, lam, tuple(res[m] * (s_in[chip, m] + s_got[m]) for m in range(order)))
    gate_out(gated.at[me], q_ref, k_ref, v_ref, skip_ref, x_ref)

    def same_core(d):
        return flip(chip, d) * 2 + core

    def other_core(d):
        return flip(chip, d) * 2 + 1 - core

    def part_of(e):
        return pl.ds(e * half, half)

    def gated_copy(index, slot, e, send):
        block = gated.at[slot, part_of(e)]
        return over("ctx", index, block, block, send, g_recv.at[slot, e])

    def first_copy(d, e):
        return gated_copy(sib if d == 0 else same_core(d), me, e, g_send.at[d, e])

    def forward_copy(d, e):
        return gated_copy(sib, same_core(d), e, f_send.at[d, e])

    def relay_copy(index, slot, e, part):
        block = gated.at[slot, pl.ds(e * half + part * quarter, quarter)]
        return over("ctx", index, block, block, h_send.at[e, part], h_recv.at[e, part])

    def product(i, e):
        return jnp.dot(gated[i, part_of(e)], w_ref[...], preferred_element_type=F32).astype(BF16)

    def back_copy(i, slot, e):
        return over(
            "ctx", i, share.at[i, part_of(e)], cols_in.at[slot, part_of(e)],
            p_send.at[i, e], p_recv.at[slot, e],
        )

    def sum_copy(k, source, e):
        return over(
            "tp", k // per_tp, cols_in.at[k, part_of(e)], sums_in.at[source, k % per_tp, part_of(e)],
            z_send.at[k, e], z_recv.at[source, k % per_tp, e],
        )

    def send_back(i, e):
        share[i, part_of(e)] = product(i, e)
        back_copy(i, me, e).start()

    def send_on(k, e):
        @pl.when(k // per_tp != row)
        def _():
            sum_copy(k, row, e).start()

    def arrived(k, e):
        back_copy(k, k, e).wait_recv()
        send_on(k, e)

    def take_sib(e):
        gated_copy(sib, sib, e, g_send.at[0, e]).wait_recv()
        send_back(sib, e)

    def receive_same(d, e):
        i = same_core(d)
        gated_copy(i, i, e, g_send.at[d, e]).wait_recv()
        relay_copy(same_core(3 - d), i, e, 2 - d).start()
        forward_copy(d, e).start()

    def take_same(d, e):
        receive_same(d, e)
        send_back(same_core(d), e)

    def receive_far(e):
        i = same_core(3)
        relay_copy(me, i, e, 0).wait_recv()
        relay_copy(me, i, e, 1).wait_recv()
        forward_copy(3, e).start()

    def take_far(e):
        receive_far(e)
        send_back(same_core(3), e)

    def receive_other(d, e):
        gated_copy(sib, other_core(d), e, f_send.at[d, e]).wait_recv()

    def take_other(d, e):
        receive_other(d, e)
        send_back(other_core(d), e)

    def send_first(e):
        first_copy(1, e).start()
        first_copy(2, e).start()
        first_copy(0, e).start()
        cols_in[me, part_of(e)] = product(me, e)
        send_on(me, e)

    send_first(0)
    take_sib(0)
    for d in range(chips - 1):
        first_copy(d, 0).wait_send()
    send_first(1)
    take_same(1, 0)
    take_same(2, 0)
    arrived(sib, 0)
    take_sib(1)
    take_other(1, 0)
    take_other(2, 0)
    take_far(0)
    arrived(same_core(1), 0)
    arrived(same_core(2), 0)
    receive_same(1, 1)
    receive_same(2, 1)
    send_back(same_core(1), 1)
    take_other(3, 0)
    arrived(other_core(1), 0)
    arrived(other_core(2), 0)
    arrived(sib, 1)
    take_other(1, 1)
    receive_far(1)
    even = row % 2 == 0
    near_pair = (same_core(2), other_core(2))
    far_pair = (same_core(3), other_core(3))
    third = [jnp.where(even, a, b) for a, b in zip(near_pair, far_pair)]
    fourth = [jnp.where(even, b, a) for a, b in zip(near_pair, far_pair)]
    send_back(third[0], 1)
    arrived(same_core(3), 0)
    receive_other(2, 1)
    receive_other(3, 1)
    send_back(third[1], 1)
    send_back(fourth[0], 1)
    send_back(fourth[1], 1)
    arrived(other_core(3), 0)
    arrived(same_core(1), 1)
    arrived(other_core(1), 1)
    for k in third + fourth:
        arrived(k, 1)

    width = w_ref.shape[1]
    for e in range(2):
        for h in range(per_tp):
            total = cols_in[row * per_tp + h, part_of(e)].astype(F32)
            for d in range(1, tp):
                source = (row + d) % tp
                sum_copy(row * per_tp + h, source, e).wait_recv()
                total = total + sums_in[source, h, part_of(e)].astype(F32)
            out_ref[part_of(e), pl.ds(h * width, width)] = total

    carry_copy.wait_send()
    for d in range(1, chips):
        state_copy(d, chip).wait_send()
    for d in range(chips - 1):
        first_copy(d, 1).wait_send()
    for e in range(2):
        for d in range(1, chips):
            forward_copy(d, e).wait_send()
        for d in (1, 2):
            relay_copy(same_core(3 - d), same_core(d), e, 2 - d).wait_send()
        for d in range(1, n):
            back_copy((me + d) % n, me, e).wait_send()
        for k in range(n):
            @pl.when(k // per_tp != row)
            def _():
                sum_copy(k, row, e).wait_send()


def fused(n, tp, query, keys, values, residues, rates, skip_gain, w_out):
    tok, chans = query.shape
    order = residues.shape[1]
    width = w_out.shape[1]
    per_tp = n // tp
    poles = (order, chans // LANES, LANES)
    dma = pltpu.SemaphoreType.DMA
    vmem = pltpu.VMEM
    blocks = vmem((n, tok, width), BF16)
    return pl.pallas_call(
        functools.partial(fused_kernel, n, tp),
        out_shape=jax.ShapeDtypeStruct((tok, per_tp * width), F32),
        in_specs=[pl.BlockSpec(memory_space=pltpu.HBM)] * 7,
        out_specs=pl.BlockSpec(memory_space=pltpu.VMEM),
        scratch_shapes=[
            vmem((tok, chans), BF16), vmem((tok, chans), BF16), vmem((tok, chans), BF16),
            vmem((order, chans), F32), vmem((order, chans), F32), vmem((1, chans), F32),
            vmem((chans, width), BF16),
            vmem((tok,) + poles[1:], F32),
            vmem(poles, F32), vmem(poles, F32), vmem(poles, F32),
            vmem((n // 2,) + poles, F32), vmem(poles, F32), vmem(poles, F32),
            vmem((n, tok, chans), BF16),
            blocks, blocks, vmem((tp, per_tp, tok, width), BF16),
            dma((7,)), dma((n // 2,)), dma((n // 2,)), dma, dma, dma((3, 2)), dma((n, 2)), dma((n // 2, 2)),
            dma((2, 2)), dma((2, 2)), dma((n, 2)), dma((n, 2)), dma((n, 2)), dma((tp, per_tp, 2)),
        ],
        compiler_params=pltpu.CompilerParams(
            collective_id=0, has_side_effects=True, vmem_limit_bytes=60 * 2**20
        ),
    )(query, keys, values, residues.T, rates.T, skip_gain[None, :], w_out).astype(BF16)


def states_kernel(k_ref, v_ref, rate_ref, s_ref, x_ref, lam):
    spread_channels(x_ref, gate_in(k_ref, v_ref).astype(F32))
    spread_channels(lam, rate_ref[...])
    zero = tuple(jnp.zeros(lam.shape[1:], F32) for _ in range(lam.shape[0]))
    state = run_states(x_ref, lam, zero)
    for m in range(lam.shape[0]):
        s_ref[m] = state[m]


def conv_kernel(q_ref, k_ref, v_ref, res_ref, rate_ref, skip_ref, s_ref, out_ref, x_ref, lam, res):
    spread_channels(x_ref, gate_in(k_ref, v_ref).astype(F32))
    spread_channels(lam, rate_ref[...])
    spread_channels(res, res_ref[...])
    run_conv(x_ref, lam, res, tuple(s_ref[m] for m in range(lam.shape[0])))
    gate_out(out_ref, q_ref, k_ref, v_ref, skip_ref, x_ref)


def gathered(n, query, keys, values, residues, rates, skip_gain, w_out):
    tok, chans = query.shape
    order = residues.shape[1]
    poles = (order, chans // LANES, LANES)
    block = (tok,) + poles[1:]
    vmem = pl.BlockSpec(memory_space=pltpu.VMEM)
    state = pl.pallas_call(
        states_kernel,
        out_shape=jax.ShapeDtypeStruct(poles, F32),
        in_specs=[vmem] * 3,
        out_specs=vmem,
        scratch_shapes=[pltpu.VMEM(block, F32), pltpu.VMEM(poles, F32)],
        compiler_params=pltpu.CompilerParams(vmem_limit_bytes=24 * 2**20),
    )(keys, values, rates.T)
    me = lax.axis_index("ctx")
    lam = rates.T.reshape(poles)
    blocks = lax.all_gather(state, "ctx")
    away = me - 1 - jnp.arange(n, dtype=jnp.int32)
    steps = (jnp.maximum(away, 0) * tok).astype(F32)[:, None, None, None]
    live = (away >= 0)[:, None, None, None]
    carry = jnp.sum(jnp.where(live, jnp.exp(-lam[None] * steps) * blocks, 0.0), axis=0)
    gated = pl.pallas_call(
        conv_kernel,
        out_shape=jax.ShapeDtypeStruct((tok, chans), BF16),
        in_specs=[vmem] * 7,
        out_specs=vmem,
        scratch_shapes=[pltpu.VMEM(block, F32), pltpu.VMEM(poles, F32), pltpu.VMEM(poles, F32)],
        compiler_params=pltpu.CompilerParams(vmem_limit_bytes=24 * 2**20),
    )(query, keys, values, residues.T, rates.T, skip_gain[None, :], carry)
    weights = lax.all_gather(w_out, "ctx", axis=1, tiled=True)
    part = jnp.dot(gated, weights, preferred_element_type=F32).astype(BF16)
    return lax.psum_scatter(part, "tp", scatter_dimension=1, tiled=True)


def solution(mesh):
    n, tp = mesh.shape["ctx"], mesh.shape["tp"]

    def per_device(query, keys, values, residues, rates, skip_gain, w_out):
        args = (query, keys, values, residues, rates, skip_gain, w_out)
        few_tokens = n * query.shape[0] <= tp * query.shape[1]
        even = n == 8 and n % tp == 0 and w_out.shape[1] % LANES == 0 and query.shape[0] % 64 == 0
        if few_tokens and even:
            return fused(n, tp, *args)
        return gathered(n, *args)

    placed = (
        P("ctx", "tp"),
        P("ctx", "tp"),
        P("ctx", "tp"),
        P("tp", None),
        P("tp", None),
        P("tp"),
        P("tp", "ctx"),
    )
    return jax.shard_map(
        per_device, mesh=mesh, in_specs=placed, out_specs=P("ctx", "tp"), check_vma=False
    )
```

```python
import functools

import jax
import jax.numpy as jnp
from jax import lax
from jax.experimental import pallas as pl
from jax.experimental.pallas import tpu as pltpu
from jax.sharding import PartitionSpec as P

MESH = pl.DeviceIdType.MESH
LANES = 128
F32 = jnp.float32
BF16 = jnp.bfloat16


def spread_channels(dst, value):
    for j in range(value.shape[1] // LANES):
        dst[:, j, :] = value[:, j * LANES : (j + 1) * LANES]


def gate_in(keys, values):
    return (keys[...].astype(F32) * values[...].astype(F32)).astype(BF16)


def tree_sum(terms):
    terms = list(terms)
    while len(terms) > 1:
        odd = [terms[-1]] if len(terms) % 2 else []
        terms = [terms[i] + terms[i + 1] for i in range(0, len(terms) - 1, 2)] + odd
    return terms[0]


def run_states(x_ref, lam, start, unroll=8):
    order = lam.shape[0]
    decay = [jnp.exp(-lam[m]) for m in range(order)]

    def body(t, state):
        for u in range(unroll):
            token = x_ref[t * unroll + u]
            state = tuple(decay[m] * state[m] + token for m in range(order))
        return state

    return lax.fori_loop(0, x_ref.shape[0] // unroll, body, start)


def run_conv(x_ref, lam, res, start, unroll=4):
    order = lam.shape[0]
    decay = [jnp.exp(-lam[m]) for m in range(order)]

    def body(t, state):
        for u in range(unroll):
            token = x_ref[t * unroll + u]
            state = tuple(decay[m] * state[m] + token for m in range(order))
            x_ref[t * unroll + u] = tree_sum([res[m] * state[m] for m in range(order)])
        return state

    lax.fori_loop(0, x_ref.shape[0] // unroll, body, start)


def add_carry(y_ref, lam, start, unroll=8):
    order = lam.shape[0]
    decay = [jnp.exp(-lam[m]) for m in range(order)]

    def body(t, state):
        for u in range(unroll):
            state = tuple(decay[m] * state[m] for m in range(order))
            y_ref[t * unroll + u] = y_ref[t * unroll + u] + tree_sum(state)
        return state

    lax.fori_loop(0, y_ref.shape[0] // unroll, body, start)


def gate_out(dst, q_ref, k_ref, v_ref, skip_ref, y_ref):
    for j in range(q_ref.shape[1] // LANES):
        cols = pl.ds(j * LANES, LANES)
        gated_in = (k_ref[:, cols].astype(F32) * v_ref[:, cols].astype(F32)).astype(BF16)
        conv = y_ref[:, j, :].astype(BF16).astype(F32)
        total = conv + skip_ref[:, cols] * gated_in.astype(F32)
        dst[:, cols] = (q_ref[:, cols].astype(F32) * total).astype(BF16)


def flip(number, bits):
    for b in range(bits.bit_length()):
        if bits >> b & 1:
            number = number + (1 << b) - 2 * (1 << b) * (number // (1 << b) % 2)
    return number


def fused_kernel(
    n, tp, q_hbm, k_hbm, v_hbm, res_hbm, rate_hbm, skip_hbm, w_hbm, out_ref,
    q_ref, k_ref, v_ref, res_ref, rate_ref, skip_ref, w_ref,
    x_ref, lam, res, s_own, s_in, s_give, s_got, gated, share, cols_in, sums_in,
    load, s_send, s_recv, c_send, c_recv, g_send, g_recv, f_send, h_send, h_recv,
    p_send, p_recv, z_send, z_recv,
):
    me = lax.axis_index("ctx")
    row = lax.axis_index("tp")
    core = me % 2
    chip = me // 2
    sib = me + 1 - 2 * core
    chips = n // 2
    per_tp = n // tp
    tok = q_ref.shape[0]
    half = tok // 2
    quarter = tok // 4
    order = lam.shape[0]
    shape = lam.shape[1:]

    pairs = (
        (k_hbm, k_ref), (v_hbm, v_ref), (rate_hbm, rate_ref), (res_hbm, res_ref),
        (q_hbm, q_ref), (skip_hbm, skip_ref), (w_hbm, w_ref),
    )
    loads = [pltpu.make_async_copy(src, dst, load.at[i]) for i, (src, dst) in enumerate(pairs)]
    for copy in loads:
        copy.start()

    barrier = pltpu.get_barrier_semaphore()
    for d in range(1, n):
        pl.semaphore_signal(barrier, inc=1, device_id={"ctx": (me + d) % n}, device_id_type=MESH)

    for d in range(1, tp):
        pl.semaphore_signal(barrier, inc=1, device_id={"tp": (row + d) % tp}, device_id_type=MESH)

    for copy in loads[:3]:
        copy.wait()
    spread_channels(x_ref, gate_in(k_ref, v_ref).astype(F32))
    spread_channels(lam, rate_ref[...])
    zero = tuple(jnp.zeros(shape, F32) for _ in range(order))
    state = run_states(x_ref, lam, zero)
    for m in range(order):
        s_own[m] = state[m]

    pl.semaphore_wait(barrier, n - 1 + tp - 1)

    def over(axis, index, src, dst, send, recv):
        return pltpu.make_async_remote_copy(
            src_ref=src, dst_ref=dst, send_sem=send, recv_sem=recv,
            device_id={axis: index}, device_id_type=MESH,
        )

    def state_copy(d, slot):
        return over("ctx", flip(chip, d) * 2 + core, s_own, s_in.at[slot], s_send.at[d], s_recv.at[slot])

    for d in range(1, chips):
        state_copy(d, chip).start()
    loads[3].wait()
    spread_channels(res, res_ref[...])
    run_conv(x_ref, lam, res, zero)
    for copy in loads[4:]:
        copy.wait()
    for d in range(1, chips):
        state_copy(d, flip(chip, d)).wait_recv()

    def carry_for(target, dst):
        def weight(source):
            steps = (jnp.maximum(target - 1 - source, 0) * tok).astype(F32)
            live = jnp.where(source < target, 1.0, 0.0).astype(F32)
            return steps, live

        weights = [weight(me)] + [weight(flip(chip, d) * 2 + core) for d in range(1, chips)]
        for m in range(order):
            total = jnp.zeros(shape, F32)
            for d in range(chips):
                part = s_own[m] if d == 0 else s_in[flip(chip, d), m]
                total = total + jnp.exp(-lam[m] * weights[d][0]) * weights[d][1] * part
            dst[m] = total

    carry_for(sib, s_give)
    carry_copy = over("ctx", sib, s_give, s_got, c_send, c_recv)
    carry_copy.start()
    carry_for(me, s_in.at[chip])
    carry_copy.wait_recv()
    add_carry(x_ref, lam, tuple(res[m] * (s_in[chip, m] + s_got[m]) for m in range(order)))
    gate_out(gated.at[me], q_ref, k_ref, v_ref, skip_ref, x_ref)

    def same_core(d):
        return flip(chip, d) * 2 + core

    def other_core(d):
        return flip(chip, d) * 2 + 1 - core

    def part_of(e):
        return pl.ds(e * half, half)

    def gated_copy(index, slot, e, send):
        block = gated.at[slot, part_of(e)]
        return over("ctx", index, block, block, send, g_recv.at[slot, e])

    def first_copy(d, e):
        return gated_copy(sib if d == 0 else same_core(d), me, e, g_send.at[d, e])

    def forward_copy(d, e):
        return gated_copy(sib, same_core(d), e, f_send.at[d, e])

    def relay_copy(index, slot, e, part):
        block = gated.at[slot, pl.ds(e * half + part * quarter, quarter)]
        return over("ctx", index, block, block, h_send.at[e, part], h_recv.at[e, part])

    def product(i, e):
        return jnp.dot(gated[i, part_of(e)], w_ref[...], preferred_element_type=F32).astype(BF16)

    def back_copy(i, slot, e):
        return over(
            "ctx", i, share.at[i, part_of(e)], cols_in.at[slot, part_of(e)],
            p_send.at[i, e], p_recv.at[slot, e],
        )

    def sum_copy(k, source, e):
        return over(
            "tp", k // per_tp, cols_in.at[k, part_of(e)], sums_in.at[source, k % per_tp, part_of(e)],
            z_send.at[k, e], z_recv.at[source, k % per_tp, e],
        )

    def send_back(i, e):
        share[i, part_of(e)] = product(i, e)
        back_copy(i, me, e).start()

    def send_back_pair(i, j, e):
        rows = jnp.concatenate([gated[i, part_of(e)], gated[j, part_of(e)]], axis=0)
        result = jnp.dot(rows, w_ref[...], preferred_element_type=F32).astype(BF16)
        share[i, part_of(e)] = result[:half]
        back_copy(i, me, e).start()
        share[j, part_of(e)] = result[half:]
        back_copy(j, me, e).start()

    def send_on(k, e):
        @pl.when(k // per_tp != row)
        def _():
            sum_copy(k, row, e).start()

    def arrived(k, e):
        back_copy(k, k, e).wait_recv()
        send_on(k, e)

    def take_sib(e):
        gated_copy(sib, sib, e, g_send.at[0, e]).wait_recv()
        send_back(sib, e)

    def receive_same(d, e):
        i = same_core(d)
        gated_copy(i, i, e, g_send.at[d, e]).wait_recv()
        relay_copy(same_core(3 - d), i, e, 2 - d).start()
        forward_copy(d, e).start()

    def receive_far(e):
        i = same_core(3)
        relay_copy(me, i, e, 0).wait_recv()
        relay_copy(me, i, e, 1).wait_recv()
        forward_copy(3, e).start()

    def take_far(e):
        receive_far(e)
        send_back(same_core(3), e)

    def receive_other(d, e):
        gated_copy(sib, other_core(d), e, f_send.at[d, e]).wait_recv()

    def take_other(d, e):
        receive_other(d, e)
        send_back(other_core(d), e)

    def send_first(e):
        first_copy(1, e).start()
        first_copy(2, e).start()
        first_copy(0, e).start()
        cols_in[me, part_of(e)] = product(me, e)
        send_on(me, e)

    send_first(0)
    take_sib(0)
    for d in range(chips - 1):
        first_copy(d, 0).wait_send()
    send_first(1)
    receive_same(1, 0)
    receive_same(2, 0)
    send_back_pair(same_core(1), same_core(2), 0)
    arrived(sib, 0)
    take_sib(1)
    receive_other(1, 0)
    receive_other(2, 0)
    send_back_pair(other_core(1), other_core(2), 0)
    take_far(0)
    arrived(same_core(1), 0)
    arrived(same_core(2), 0)
    receive_same(1, 1)
    receive_same(2, 1)
    send_back(same_core(1), 1)
    take_other(3, 0)
    arrived(other_core(1), 0)
    arrived(other_core(2), 0)
    arrived(sib, 1)
    take_other(1, 1)
    receive_far(1)
    even = row % 2 == 0
    near_pair = (same_core(2), other_core(2))
    far_pair = (same_core(3), other_core(3))
    third = [jnp.where(even, a, b) for a, b in zip(near_pair, far_pair)]
    fourth = [jnp.where(even, b, a) for a, b in zip(near_pair, far_pair)]
    send_back(third[0], 1)
    arrived(same_core(3), 0)
    receive_other(2, 1)
    receive_other(3, 1)
    send_back(third[1], 1)
    send_back_pair(fourth[0], fourth[1], 1)
    arrived(other_core(3), 0)
    arrived(same_core(1), 1)
    arrived(other_core(1), 1)
    for k in third + fourth:
        arrived(k, 1)

    width = w_ref.shape[1]
    for e in range(2):
        for h in range(per_tp):
            total = cols_in[row * per_tp + h, part_of(e)].astype(F32)
            for d in range(1, tp):
                source = (row + d) % tp
                sum_copy(row * per_tp + h, source, e).wait_recv()
                total = total + sums_in[source, h, part_of(e)].astype(F32)
            out_ref[part_of(e), pl.ds(h * width, width)] = total.astype(BF16)

    carry_copy.wait_send()
    for d in range(1, chips):
        state_copy(d, chip).wait_send()
    for d in range(chips - 1):
        first_copy(d, 1).wait_send()
    for e in range(2):
        for d in range(1, chips):
            forward_copy(d, e).wait_send()
        for d in (1, 2):
            relay_copy(same_core(3 - d), same_core(d), e, 2 - d).wait_send()
        for d in range(1, n):
            back_copy((me + d) % n, me, e).wait_send()
        for k in range(n):
            @pl.when(k // per_tp != row)
            def _():
                sum_copy(k, row, e).wait_send()


def fused(n, tp, query, keys, values, residues, rates, skip_gain, w_out):
    tok, chans = query.shape
    order = residues.shape[1]
    width = w_out.shape[1]
    per_tp = n // tp
    poles = (order, chans // LANES, LANES)
    dma = pltpu.SemaphoreType.DMA
    vmem = pltpu.VMEM
    blocks = vmem((n, tok, width), BF16)
    return pl.pallas_call(
        functools.partial(fused_kernel, n, tp),
        out_shape=jax.ShapeDtypeStruct((tok, per_tp * width), BF16),
        in_specs=[pl.BlockSpec(memory_space=pltpu.HBM)] * 7,
        out_specs=pl.BlockSpec(memory_space=pltpu.VMEM),
        scratch_shapes=[
            vmem((tok, chans), BF16), vmem((tok, chans), BF16), vmem((tok, chans), BF16),
            vmem((order, chans), F32), vmem((order, chans), F32), vmem((1, chans), F32),
            vmem((chans, width), BF16),
            vmem((tok,) + poles[1:], F32),
            vmem(poles, F32), vmem(poles, F32), vmem(poles, F32),
            vmem((n // 2,) + poles, F32), vmem(poles, F32), vmem(poles, F32),
            vmem((n, tok, chans), BF16),
            blocks, blocks, vmem((tp, per_tp, tok, width), BF16),
            dma((7,)), dma((n // 2,)), dma((n // 2,)), dma, dma, dma((3, 2)), dma((n, 2)), dma((n // 2, 2)),
            dma((2, 2)), dma((2, 2)), dma((n, 2)), dma((n, 2)), dma((n, 2)), dma((tp, per_tp, 2)),
        ],
        compiler_params=pltpu.CompilerParams(
            collective_id=0, has_side_effects=True, vmem_limit_bytes=107 * 2**19
        ),
    )(query, keys, values, residues.T, rates.T, skip_gain[None, :], w_out)


def states_kernel(k_ref, v_ref, rate_ref, s_ref, x_ref, lam):
    spread_channels(x_ref, gate_in(k_ref, v_ref).astype(F32))
    spread_channels(lam, rate_ref[...])
    zero = tuple(jnp.zeros(lam.shape[1:], F32) for _ in range(lam.shape[0]))
    state = run_states(x_ref, lam, zero)
    for m in range(lam.shape[0]):
        s_ref[m] = state[m]


def conv_kernel(q_ref, k_ref, v_ref, res_ref, rate_ref, skip_ref, s_ref, out_ref, x_ref, lam, res):
    spread_channels(x_ref, gate_in(k_ref, v_ref).astype(F32))
    spread_channels(lam, rate_ref[...])
    spread_channels(res, res_ref[...])
    run_conv(x_ref, lam, res, tuple(s_ref[m] for m in range(lam.shape[0])))
    gate_out(out_ref, q_ref, k_ref, v_ref, skip_ref, x_ref)


def gathered(n, query, keys, values, residues, rates, skip_gain, w_out):
    tok, chans = query.shape
    order = residues.shape[1]
    poles = (order, chans // LANES, LANES)
    block = (tok,) + poles[1:]
    vmem = pl.BlockSpec(memory_space=pltpu.VMEM)
    state = pl.pallas_call(
        states_kernel,
        out_shape=jax.ShapeDtypeStruct(poles, F32),
        in_specs=[vmem] * 3,
        out_specs=vmem,
        scratch_shapes=[pltpu.VMEM(block, F32), pltpu.VMEM(poles, F32)],
        compiler_params=pltpu.CompilerParams(vmem_limit_bytes=24 * 2**20),
    )(keys, values, rates.T)
    me = lax.axis_index("ctx")
    lam = rates.T.reshape(poles)
    blocks = lax.all_gather(state, "ctx")
    away = me - 1 - jnp.arange(n, dtype=jnp.int32)
    steps = (jnp.maximum(away, 0) * tok).astype(F32)[:, None, None, None]
    live = (away >= 0)[:, None, None, None]
    carry = jnp.sum(jnp.where(live, jnp.exp(-lam[None] * steps) * blocks, 0.0), axis=0)
    gated = pl.pallas_call(
        conv_kernel,
        out_shape=jax.ShapeDtypeStruct((tok, chans), BF16),
        in_specs=[vmem] * 7,
        out_specs=vmem,
        scratch_shapes=[pltpu.VMEM(block, F32), pltpu.VMEM(poles, F32), pltpu.VMEM(poles, F32)],
        compiler_params=pltpu.CompilerParams(vmem_limit_bytes=24 * 2**20),
    )(query, keys, values, residues.T, rates.T, skip_gain[None, :], carry)
    weights = lax.all_gather(w_out, "ctx", axis=1, tiled=True)
    part = jnp.dot(gated, weights, preferred_element_type=F32).astype(BF16)
    return lax.psum_scatter(part, "tp", scatter_dimension=1, tiled=True)


def solution(mesh):
    n, tp = mesh.shape["ctx"], mesh.shape["tp"]

    def per_device(query, keys, values, residues, rates, skip_gain, w_out):
        args = (query, keys, values, residues, rates, skip_gain, w_out)
        few_tokens = n * query.shape[0] <= tp * query.shape[1]
        even = n == 8 and n % tp == 0 and w_out.shape[1] % LANES == 0 and query.shape[0] % 64 == 0
        if few_tokens and even:
            return fused(n, tp, *args)
        return gathered(n, *args)

    placed = (
        P("ctx", "tp"),
        P("ctx", "tp"),
        P("ctx", "tp"),
        P("tp", None),
        P("tp", None),
        P("tp"),
        P("tp", "ctx"),
    )
    return jax.shard_map(
        per_device, mesh=mesh, in_specs=placed, out_specs=P("ctx", "tp"), check_vma=False
    )
```

```python
import functools

import jax
import jax.numpy as jnp
from jax import lax
from jax.experimental import pallas as pl
from jax.experimental.pallas import tpu as pltpu
from jax.sharding import PartitionSpec as P

MESH = pl.DeviceIdType.MESH
LANES = 128
F32 = jnp.float32
BF16 = jnp.bfloat16


def spread_channels(dst, value):
    for j in range(value.shape[1] // LANES):
        dst[:, j, :] = value[:, j * LANES : (j + 1) * LANES]


def gate_in(keys, values):
    return (keys[...].astype(F32) * values[...].astype(F32)).astype(BF16)


def tree_sum(terms):
    terms = list(terms)
    while len(terms) > 1:
        odd = [terms[-1]] if len(terms) % 2 else []
        terms = [terms[i] + terms[i + 1] for i in range(0, len(terms) - 1, 2)] + odd
    return terms[0]


def run_states(x_ref, lam, start, unroll=8):
    order = lam.shape[0]
    decay = [jnp.exp(-lam[m]) for m in range(order)]

    def body(t, state):
        for u in range(unroll):
            token = x_ref[t * unroll + u]
            state = tuple(decay[m] * state[m] + token for m in range(order))
        return state

    return lax.fori_loop(0, x_ref.shape[0] // unroll, body, start)


def run_conv(x_ref, lam, res, start, unroll=4):
    order = lam.shape[0]
    decay = [jnp.exp(-lam[m]) for m in range(order)]

    def body(t, state):
        for u in range(unroll):
            token = x_ref[t * unroll + u]
            state = tuple(decay[m] * state[m] + token for m in range(order))
            x_ref[t * unroll + u] = tree_sum([res[m] * state[m] for m in range(order)])
        return state

    lax.fori_loop(0, x_ref.shape[0] // unroll, body, start)


def add_carry(y_ref, lam, start, unroll=8):
    order = lam.shape[0]
    decay = [jnp.exp(-lam[m]) for m in range(order)]

    def body(t, state):
        for u in range(unroll):
            state = tuple(decay[m] * state[m] for m in range(order))
            y_ref[t * unroll + u] = y_ref[t * unroll + u] + tree_sum(state)
        return state

    lax.fori_loop(0, y_ref.shape[0] // unroll, body, start)


def gate_out(dst, q_ref, k_ref, v_ref, skip_ref, y_ref):
    for j in range(q_ref.shape[1] // LANES):
        cols = pl.ds(j * LANES, LANES)
        gated_in = (k_ref[:, cols].astype(F32) * v_ref[:, cols].astype(F32)).astype(BF16)
        conv = y_ref[:, j, :].astype(BF16).astype(F32)
        total = conv + skip_ref[:, cols] * gated_in.astype(F32)
        dst[:, cols] = (q_ref[:, cols].astype(F32) * total).astype(BF16)


def flip(number, bits):
    for b in range(bits.bit_length()):
        if bits >> b & 1:
            number = number + (1 << b) - 2 * (1 << b) * (number // (1 << b) % 2)
    return number


def fused_kernel(
    n, tp, q_hbm, k_hbm, v_hbm, res_hbm, rate_hbm, skip_hbm, w_hbm, out_ref,
    q_ref, k_ref, v_ref, res_ref, rate_ref, skip_ref, w_ref,
    x_ref, lam, res, s_own, s_in, s_give, s_got, gated, share, cols_in, sums_in,
    load, s_send, s_recv, c_send, c_recv, g_send, g_recv, f_send, h_send, h_recv,
    p_send, p_recv, z_send, z_recv,
):
    me = lax.axis_index("ctx")
    row = lax.axis_index("tp")
    core = me % 2
    chip = me // 2
    sib = me + 1 - 2 * core
    chips = n // 2
    per_tp = n // tp
    tok = q_ref.shape[0]
    half = tok // 2
    quarter = tok // 4
    order = lam.shape[0]
    shape = lam.shape[1:]

    pairs = (
        (k_hbm, k_ref), (v_hbm, v_ref), (rate_hbm, rate_ref), (res_hbm, res_ref),
        (q_hbm, q_ref), (skip_hbm, skip_ref), (w_hbm, w_ref),
    )
    loads = [pltpu.make_async_copy(src, dst, load.at[i]) for i, (src, dst) in enumerate(pairs)]
    for copy in loads:
        copy.start()

    barrier = pltpu.get_barrier_semaphore()
    for d in range(1, n):
        pl.semaphore_signal(barrier, inc=1, device_id={"ctx": (me + d) % n}, device_id_type=MESH)

    for d in range(1, tp):
        pl.semaphore_signal(barrier, inc=1, device_id={"tp": (row + d) % tp}, device_id_type=MESH)

    for copy in loads[:3]:
        copy.wait()
    spread_channels(x_ref, gate_in(k_ref, v_ref).astype(F32))
    spread_channels(lam, rate_ref[...])
    zero = tuple(jnp.zeros(shape, F32) for _ in range(order))
    state = run_states(x_ref, lam, zero)
    for m in range(order):
        s_own[m] = state[m]

    pl.semaphore_wait(barrier, n - 1 + tp - 1)

    def over(axis, index, src, dst, send, recv):
        return pltpu.make_async_remote_copy(
            src_ref=src, dst_ref=dst, send_sem=send, recv_sem=recv,
            device_id={axis: index}, device_id_type=MESH,
        )

    def state_copy(d, slot):
        return over("ctx", flip(chip, d) * 2 + core, s_own, s_in.at[slot], s_send.at[d], s_recv.at[slot])

    for d in range(1, chips):
        state_copy(d, chip).start()
    loads[3].wait()
    spread_channels(res, res_ref[...])
    run_conv(x_ref, lam, res, zero)
    for copy in loads[4:]:
        copy.wait()
    for d in range(1, chips):
        state_copy(d, flip(chip, d)).wait_recv()

    def carry_for(target, dst):
        def weight(source):
            steps = (jnp.maximum(target - 1 - source, 0) * tok).astype(F32)
            live = jnp.where(source < target, 1.0, 0.0).astype(F32)
            return steps, live

        weights = [weight(me)] + [weight(flip(chip, d) * 2 + core) for d in range(1, chips)]
        for m in range(order):
            total = jnp.zeros(shape, F32)
            for d in range(chips):
                part = s_own[m] if d == 0 else s_in[flip(chip, d), m]
                total = total + jnp.exp(-lam[m] * weights[d][0]) * weights[d][1] * part
            dst[m] = total

    carry_for(sib, s_give)
    carry_copy = over("ctx", sib, s_give, s_got, c_send, c_recv)
    carry_copy.start()
    carry_for(me, s_in.at[chip])
    carry_copy.wait_recv()
    add_carry(x_ref, lam, tuple(res[m] * (s_in[chip, m] + s_got[m]) for m in range(order)))
    gate_out(gated.at[me], q_ref, k_ref, v_ref, skip_ref, x_ref)

    def same_core(d):
        return flip(chip, d) * 2 + core

    def other_core(d):
        return flip(chip, d) * 2 + 1 - core

    def part_of(e):
        return pl.ds(e * half, half)

    def gated_copy(index, slot, e, send):
        block = gated.at[slot, part_of(e)]
        return over("ctx", index, block, block, send, g_recv.at[slot, e])

    def first_copy(d, e):
        return gated_copy(sib if d == 0 else same_core(d), me, e, g_send.at[d, e])

    def forward_copy(d, e):
        return gated_copy(sib, same_core(d), e, f_send.at[d, e])

    def relay_copy(index, slot, e, part):
        block = gated.at[slot, pl.ds(e * half + part * quarter, quarter)]
        return over("ctx", index, block, block, h_send.at[e, part], h_recv.at[e, part])

    def product(i, e):
        return jnp.dot(gated[i, part_of(e)], w_ref[...], preferred_element_type=F32).astype(BF16)

    def back_copy(i, slot, e):
        return over(
            "ctx", i, share.at[i, part_of(e)], cols_in.at[slot, part_of(e)],
            p_send.at[i, e], p_recv.at[slot, e],
        )

    def sum_copy(k, source, e):
        return over(
            "tp", k // per_tp, cols_in.at[k, part_of(e)], sums_in.at[source, k % per_tp, part_of(e)],
            z_send.at[k, e], z_recv.at[source, k % per_tp, e],
        )

    def send_back(i, e):
        share[i, part_of(e)] = product(i, e)
        back_copy(i, me, e).start()

    def send_back_pair(i, j, e):
        rows = jnp.concatenate([gated[i, part_of(e)], gated[j, part_of(e)]], axis=0)
        result = jnp.dot(rows, w_ref[...], preferred_element_type=F32).astype(BF16)
        share[i, part_of(e)] = result[:half]
        back_copy(i, me, e).start()
        share[j, part_of(e)] = result[half:]
        back_copy(j, me, e).start()

    def send_on(k, e):
        @pl.when(k // per_tp != row)
        def _():
            sum_copy(k, row, e).start()

    def arrived(k, e):
        back_copy(k, k, e).wait_recv()
        send_on(k, e)

    def take_sib(e):
        gated_copy(sib, sib, e, g_send.at[0, e]).wait_recv()
        send_back(sib, e)

    def receive_same(d, e):
        i = same_core(d)
        gated_copy(i, i, e, g_send.at[d, e]).wait_recv()
        relay_copy(same_core(3 - d), i, e, 2 - d).start()
        forward_copy(d, e).start()

    def receive_far(e):
        i = same_core(3)
        relay_copy(me, i, e, 0).wait_recv()
        relay_copy(me, i, e, 1).wait_recv()
        forward_copy(3, e).start()

    def take_far(e):
        receive_far(e)
        send_back(same_core(3), e)

    def receive_other(d, e):
        gated_copy(sib, other_core(d), e, f_send.at[d, e]).wait_recv()

    def take_other(d, e):
        receive_other(d, e)
        send_back(other_core(d), e)

    def send_first(e):
        first_copy(1, e).start()
        first_copy(2, e).start()
        first_copy(0, e).start()
        cols_in[me, part_of(e)] = product(me, e)
        send_on(me, e)

    send_first(0)
    take_sib(0)
    for d in range(chips - 1):
        first_copy(d, 0).wait_send()
    send_first(1)
    receive_same(1, 0)
    receive_same(2, 0)
    send_back_pair(same_core(1), same_core(2), 0)
    arrived(sib, 0)
    take_sib(1)
    receive_other(1, 0)
    receive_other(2, 0)
    send_back_pair(other_core(1), other_core(2), 0)
    take_far(0)
    arrived(same_core(1), 0)
    arrived(same_core(2), 0)
    receive_same(1, 1)
    receive_same(2, 1)
    send_back(same_core(1), 1)
    take_other(3, 0)
    arrived(other_core(1), 0)
    arrived(other_core(2), 0)
    arrived(sib, 1)
    take_other(1, 1)
    receive_far(1)
    even = row % 2 == 0
    near_pair = (same_core(2), other_core(2))
    far_pair = (same_core(3), other_core(3))
    third = [jnp.where(even, a, b) for a, b in zip(near_pair, far_pair)]
    fourth = [jnp.where(even, b, a) for a, b in zip(near_pair, far_pair)]
    send_back(third[0], 1)
    arrived(same_core(3), 0)
    receive_other(2, 1)
    receive_other(3, 1)
    send_back(third[1], 1)
    send_back_pair(fourth[0], fourth[1], 1)
    arrived(other_core(3), 0)
    arrived(same_core(1), 1)
    arrived(other_core(1), 1)
    for k in third + fourth:
        arrived(k, 1)

    width = w_ref.shape[1]
    for e in range(2):
        for h in range(per_tp):
            total = cols_in[row * per_tp + h, part_of(e)].astype(F32)
            for d in range(1, tp):
                source = (row + d) % tp
                sum_copy(row * per_tp + h, source, e).wait_recv()
                total = total + sums_in[source, h, part_of(e)].astype(F32)
            out_ref[part_of(e), pl.ds(h * width, width)] = total.astype(BF16)

    carry_copy.wait_send()
    for d in range(1, chips):
        state_copy(d, chip).wait_send()
    for d in range(chips - 1):
        first_copy(d, 1).wait_send()
    for e in range(2):
        for d in range(1, chips):
            forward_copy(d, e).wait_send()
        for d in (1, 2):
            relay_copy(same_core(3 - d), same_core(d), e, 2 - d).wait_send()
        for d in range(1, n):
            back_copy((me + d) % n, me, e).wait_send()
        for k in range(n):
            @pl.when(k // per_tp != row)
            def _():
                sum_copy(k, row, e).wait_send()


def fused(n, tp, query, keys, values, residues, rates, skip_gain, w_out):
    tok, chans = query.shape
    order = residues.shape[1]
    width = w_out.shape[1]
    per_tp = n // tp
    poles = (order, chans // LANES, LANES)
    dma = pltpu.SemaphoreType.DMA
    vmem = pltpu.VMEM
    blocks = vmem((n, tok, width), BF16)
    return pl.pallas_call(
        functools.partial(fused_kernel, n, tp),
        out_shape=jax.ShapeDtypeStruct((tok, per_tp * width), BF16),
        in_specs=[pl.BlockSpec(memory_space=pltpu.HBM)] * 7,
        out_specs=pl.BlockSpec(memory_space=pltpu.VMEM),
        scratch_shapes=[
            vmem((tok, chans), BF16), vmem((tok, chans), BF16), vmem((tok, chans), BF16),
            vmem((order, chans), F32), vmem((order, chans), F32), vmem((1, chans), F32),
            vmem((chans, width), BF16),
            vmem((tok,) + poles[1:], F32),
            vmem(poles, F32), vmem(poles, F32), vmem(poles, F32),
            vmem((n // 2,) + poles, F32), vmem(poles, F32), vmem(poles, F32),
            vmem((n, tok, chans), BF16),
            blocks, blocks, vmem((tp, per_tp, tok, width), BF16),
            dma((7,)), dma((n // 2,)), dma((n // 2,)), dma, dma, dma((3, 2)), dma((n, 2)), dma((n // 2, 2)),
            dma((2, 2)), dma((2, 2)), dma((n, 2)), dma((n, 2)), dma((n, 2)), dma((tp, per_tp, 2)),
        ],
        compiler_params=pltpu.CompilerParams(
            collective_id=0, has_side_effects=True, vmem_limit_bytes=60 * 2**20
        ),
    )(query, keys, values, residues.T, rates.T, skip_gain[None, :], w_out)


def states_kernel(k_ref, v_ref, rate_ref, s_ref, x_ref, lam):
    spread_channels(x_ref, gate_in(k_ref, v_ref).astype(F32))
    spread_channels(lam, rate_ref[...])
    zero = tuple(jnp.zeros(lam.shape[1:], F32) for _ in range(lam.shape[0]))
    state = run_states(x_ref, lam, zero)
    for m in range(lam.shape[0]):
        s_ref[m] = state[m]


def conv_kernel(q_ref, k_ref, v_ref, res_ref, rate_ref, skip_ref, s_ref, out_ref, x_ref, lam, res):
    spread_channels(x_ref, gate_in(k_ref, v_ref).astype(F32))
    spread_channels(lam, rate_ref[...])
    spread_channels(res, res_ref[...])
    run_conv(x_ref, lam, res, tuple(s_ref[m] for m in range(lam.shape[0])))
    gate_out(out_ref, q_ref, k_ref, v_ref, skip_ref, x_ref)


def gathered(n, query, keys, values, residues, rates, skip_gain, w_out):
    tok, chans = query.shape
    order = residues.shape[1]
    poles = (order, chans // LANES, LANES)
    block = (tok,) + poles[1:]
    vmem = pl.BlockSpec(memory_space=pltpu.VMEM)
    state = pl.pallas_call(
        states_kernel,
        out_shape=jax.ShapeDtypeStruct(poles, F32),
        in_specs=[vmem] * 3,
        out_specs=vmem,
        scratch_shapes=[pltpu.VMEM(block, F32), pltpu.VMEM(poles, F32)],
        compiler_params=pltpu.CompilerParams(vmem_limit_bytes=24 * 2**20),
    )(keys, values, rates.T)
    me = lax.axis_index("ctx")
    lam = rates.T.reshape(poles)
    blocks = lax.all_gather(state, "ctx")
    away = me - 1 - jnp.arange(n, dtype=jnp.int32)
    steps = (jnp.maximum(away, 0) * tok).astype(F32)[:, None, None, None]
    live = (away >= 0)[:, None, None, None]
    carry = jnp.sum(jnp.where(live, jnp.exp(-lam[None] * steps) * blocks, 0.0), axis=0)
    gated = pl.pallas_call(
        conv_kernel,
        out_shape=jax.ShapeDtypeStruct((tok, chans), BF16),
        in_specs=[vmem] * 7,
        out_specs=vmem,
        scratch_shapes=[pltpu.VMEM(block, F32), pltpu.VMEM(poles, F32), pltpu.VMEM(poles, F32)],
        compiler_params=pltpu.CompilerParams(vmem_limit_bytes=24 * 2**20),
    )(query, keys, values, residues.T, rates.T, skip_gain[None, :], carry)
    weights = lax.all_gather(w_out, "ctx", axis=1, tiled=True)
    part = jnp.dot(gated, weights, preferred_element_type=F32).astype(BF16)
    return lax.psum_scatter(part, "tp", scatter_dimension=1, tiled=True)


def solution(mesh):
    n, tp = mesh.shape["ctx"], mesh.shape["tp"]

    def per_device(query, keys, values, residues, rates, skip_gain, w_out):
        args = (query, keys, values, residues, rates, skip_gain, w_out)
        few_tokens = n * query.shape[0] <= tp * query.shape[1]
        even = n == 8 and n % tp == 0 and w_out.shape[1] % LANES == 0 and query.shape[0] % 64 == 0
        if few_tokens and even:
            return fused(n, tp, *args)
        return gathered(n, *args)

    placed = (
        P("ctx", "tp"),
        P("ctx", "tp"),
        P("ctx", "tp"),
        P("tp", None),
        P("tp", None),
        P("tp"),
        P("tp", "ctx"),
    )
    return jax.shard_map(
        per_device, mesh=mesh, in_specs=placed, out_specs=P("ctx", "tp"), check_vma=False
    )
```
